256 devices in a mesh: seq: 16 (over y, z_lo, core), head: 16 (over x, z_hi).
Axes of the slice: x: 4, y: 4, z: 8 (z_hi: 4, z_lo: 2; z = z_hi * 2 + z_lo), core: 2. Of those that a mesh axis runs over, the one named last changes fastest.
Arguments:
- span_x: bfloat16 [4096, 5120], P('seq', 'head'), may hold values from -6 to 6
- cand_x: bfloat16 [16, 128, 5120], P('seq', None, 'head'), may hold values from -6 to 6
- cand_len: int32 [16], P('seq'), may hold values from 32 to 128, as said below
- offset: int32 [1], replicated, may hold values from 7936 to 8192
- norm_gain: float32 [5120], replicated, may hold values from 0.1 to 1.9
- wq: bfloat16 [5120, 8192], P(None, 'head'), may hold values from -0.078125 to 0.078125
- wk: bfloat16 [5120, 1024], P(None, 'head'), may hold values from -0.078125 to 0.078125
- wv: bfloat16 [5120, 1024], P(None, 'head'), may hold values from -0.078125 to 0.078125
- q_gain: float32 [128], replicated, may hold values from 1 to 3
- k_gain: float32 [128], replicated, may hold values from 1 to 3
- wo: bfloat16 [8192, 5120], P('head'), may hold values from -0.25 to 0.25
- cache_k: bfloat16 [8192, 1024], P('seq', 'head'), may hold values from -70 to 70
- cache_v: bfloat16 [8192, 1024], P('seq', 'head'), may hold values from -6 to 6
Outputs:
- span_out: bfloat16 [4096, 5120], P('seq', 'head')
- cand_out: bfloat16 [16, 128, 5120], P('seq', None, 'head')
The draws below stay inside these ranges and needn't reach their ends.
Inputs may be any that keep to these rules, and one draw needn't show every extreme that they name: `cand_len`: each candidate's real tokens; its remaining rows are padding; some candidate has all 128. Cache slots at or after offset hold no source token and are never visible.
All inputs are finite; a program needn't handle non-finite values.
Results may differ from the reference program's by a relative error of at most 0.024.
The reference program's roundings to bfloat16 on the way count: a program that leaves them out, or rounds other values in their place, can miss the bound.
Values may be sent and summed in bfloat16 or wider, within the bound.
No kernel may reach another device: no remote copies, remote signals or barrier semaphores. Data moves between devices by JAX's collectives and lax.ppermute only.
A program may use at most 128 MiB of HBM per device.

```python
import math
import jax
import jax.numpy as jnp
from jax import lax

D = 5120
HD = 128
QH_DEV = 4
HQ = 64
KVH = 8
PRE_DEV = 512
CLEN = 128
SPAN = 4096
PREFIX = 8192
NCAND = 16
N_HEAD = 16


def draw_cache_k(key, part):
    key = jax.random.fold_in(key, 7)
    first_key = jax.random.fold_in(key, 0)
    values = jnp.clip(jax.random.normal(first_key, (PREFIX, KVH * HD), jnp.float32), -6.0, 6.0)
    return values.astype(jnp.bfloat16)


def draw_cand_len(key, part):
    key = jax.random.fold_in(key, 11)
    length_key, pick_key = jax.random.split(key)
    lengths = jax.random.randint(length_key, (NCAND,), CLEN // 4, CLEN + 1)
    chosen = jax.random.randint(pick_key, (), 0, NCAND)
    return jnp.where(jnp.arange(NCAND) == chosen, CLEN, lengths).astype(jnp.int32)


def shard_levels(own_key, extent, cuts, smallest, high):
    level, own = 1.0, jax.random.fold_in(own_key, 6)
    for position, parts in cuts:
        heights = jnp.exp(jax.random.uniform(jax.random.fold_in(own, position), (parts,), jnp.float32, smallest / len(cuts), high / len(cuts)))
        level = level * jnp.repeat(heights, extent[position] // parts).reshape([-1 if axis == position else 1 for axis in range(len(extent))])
    return level


def scatter_about(own_key, extent, scale, bound, cuts=(), held_as=jnp.bfloat16):
    values = jax.random.normal(own_key, extent, jnp.float32) * scale
    if len(cuts) > 0:
        values = shard_levels(own_key, extent, cuts, -0.22, 0.18) * values
    return jnp.clip(values, min=-bound, max=bound).astype(held_as)


def setup_inputs(seed: int = 0) -> dict:
    key_list = jax.random.split(jax.random.key(seed), 14)
    span_x = scatter_about(key_list[0], (SPAN, D), 1.0, 6.0, ((0, 16), (1, 16)))
    cand_x = scatter_about(key_list[1], (NCAND, CLEN, D), 1.0, 6.0, ((0, 16), (2, 16)))
    cand_len = draw_cand_len(jax.random.fold_in(key_list[13], 71), 0)
    offset = jax.random.randint(key_list[3], (1,), PREFIX - PRE_DEV // 2, PREFIX + 1).astype(jnp.int32)
    norm_gain = jnp.clip(1.0 + 0.18 * jax.random.normal(key_list[4], (D,), jnp.float32), 0.1, 1.9)
    wq = scatter_about(key_list[5], (D, HQ * HD), D ** -0.5, 0.078125, ((1, 16),))
    wk = scatter_about(key_list[6], (D, KVH * HD), D ** -0.5, 0.078125, ((1, 16),))
    wv = scatter_about(key_list[7], (D, KVH * HD), D ** -0.5, 0.078125, ((1, 16),))
    q_gain = jnp.clip(jnp.exp(jax.random.uniform(key_list[8], (HD,), jnp.float32, math.log(1.0), math.log(3.0))), 1.0, 3.0)
    k_gain = jnp.clip(jnp.exp(jax.random.uniform(key_list[9], (HD,), jnp.float32, math.log(1.0), math.log(3.0))), 1.0, 3.0)
    wo = scatter_about(key_list[10], (HQ * HD, D), (HQ * HD // 16) ** -0.5, 0.25, ((0, 16),))
    cache_k = draw_cache_k(jax.random.fold_in(key_list[13], 71), 0)
    cache_v = scatter_about(key_list[12], (PREFIX, KVH * HD), 1.0, 6.0, ((0, 16), (1, 16)))
    return dict(span_x=span_x, cand_x=cand_x, cand_len=cand_len, offset=offset, norm_gain=norm_gain, wq=wq, wk=wk, wv=wv, q_gain=q_gain, k_gain=k_gain, wo=wo, cache_k=cache_k, cache_v=cache_v)


epsilon = 1e-06
rope_base = 1000000.0

def rms_scale(values, gain):
    mean_square = lax.optimization_barrier(jnp.mean(values * values, axis=-1, keepdims=True))
    return values * lax.rsqrt(mean_square + epsilon) * gain

def rotate(values, positions):
    head_width = values.shape[-1]
    half_width = head_width // 2
    frequency = rope_base ** (-(jnp.arange(half_width, dtype=jnp.float32) * 2.0 / head_width))
    angles = positions.astype(jnp.float32)[:, None] * frequency[None, :]
    cosine = jnp.cos(angles)[:, None, :]
    sine_part = jnp.sin(angles)[:, None, :]
    front_half = values[..., :half_width]
    back_half = values[..., half_width:]
    return jnp.concatenate([front_half * cosine - back_half * sine_part, back_half * cosine + front_half * sine_part], axis=-1)

def reference(span_x, cand_x, cand_len, offset, norm_gain, wq, wk, wv, q_gain, k_gain, wo, cache_k, cache_v):
    span_start = offset[0]
    cand_total = NCAND * CLEN
    row_count = SPAN + cand_total
    all_rows = jnp.concatenate([span_x, cand_x.reshape(cand_total, D)], axis=0)
    positions = jnp.concatenate([span_start + jnp.arange(SPAN, dtype=jnp.int32), span_start + SPAN + jnp.tile(jnp.arange(CLEN, dtype=jnp.int32), NCAND)])
    normed = rms_scale(all_rows.astype(jnp.float32), norm_gain).astype(jnp.bfloat16)
    queries = jnp.dot(normed, wq, preferred_element_type=jnp.float32).reshape(row_count, HQ, HD)
    queries = rotate(rms_scale(queries, q_gain), positions).astype(jnp.bfloat16)
    raw_keys = jnp.dot(normed, wk, preferred_element_type=jnp.float32).astype(jnp.bfloat16).reshape(row_count, KVH, HD)
    new_keys = rotate(rms_scale(raw_keys.astype(jnp.float32), k_gain), positions).astype(jnp.bfloat16)
    new_values = jnp.dot(normed, wv, preferred_element_type=jnp.float32).astype(jnp.bfloat16).reshape(row_count, KVH, HD)
    source_keys = jnp.concatenate([cache_k.reshape(PREFIX, KVH, HD), new_keys[:SPAN]], axis=0)
    source_values = jnp.concatenate([cache_v.reshape(PREFIX, KVH, HD), new_values[:SPAN]], axis=0)
    own_keys = new_keys[SPAN:].reshape(NCAND, CLEN, KVH, HD)
    own_values = new_values[SPAN:].reshape(NCAND, CLEN, KVH, HD)
    key_pos = jnp.arange(PREFIX + SPAN, dtype=jnp.int32)
    limits = jnp.concatenate([jnp.arange(SPAN, dtype=jnp.int32), jnp.full((cand_total,), SPAN, jnp.int32)])
    visible = ((key_pos < PREFIX) & (key_pos < span_start))[None, :] | (key_pos >= PREFIX)[None, :] & ((key_pos - PREFIX)[None, :] <= limits[:, None])
    own_mask = jnp.arange(CLEN, dtype=jnp.int32)[None, :] <= jnp.arange(CLEN, dtype=jnp.int32)[:, None]
    score_scale = 1.0 / math.sqrt(HD)

    def one_head(head_idx):
        group_idx = head_idx // (HQ // KVH)
        query_head = lax.dynamic_index_in_dim(queries, head_idx, 1, False).astype(jnp.float32)
        src_keys = lax.dynamic_index_in_dim(source_keys, group_idx, 1, False).astype(jnp.float32)
        src_values = lax.dynamic_index_in_dim(source_values, group_idx, 1, False).astype(jnp.float32)
        mine_keys = lax.dynamic_index_in_dim(own_keys, group_idx, 2, False).astype(jnp.float32)
        mine_values = lax.dynamic_index_in_dim(own_values, group_idx, 2, False).astype(jnp.float32)
        scores = jnp.where(visible, jnp.dot(query_head, src_keys.T) * score_scale, -1e+30)
        cand_queries = query_head[SPAN:].reshape(NCAND, CLEN, HD)
        own_scores = jnp.einsum('cqd,ckd->cqk', cand_queries, mine_keys) * score_scale
        own_scores = jnp.where(own_mask[None], own_scores, -1e+30)
        top_src = lax.optimization_barrier(jnp.max(scores, axis=1))
        cand_top = jnp.maximum(top_src[SPAN:], lax.optimization_barrier(jnp.max(own_scores, axis=2)).reshape(cand_total))
        row_top = jnp.concatenate([top_src[:SPAN], cand_top])
        weights = jnp.where(visible, jnp.exp(scores - row_top[:, None]), 0.0)
        own_weights = jnp.where(own_mask[None], jnp.exp(own_scores - cand_top.reshape(NCAND, CLEN, 1)), 0.0)
        denominator = lax.optimization_barrier(jnp.sum(weights, axis=1)) + jnp.concatenate([jnp.zeros((SPAN,), jnp.float32), lax.optimization_barrier(jnp.sum(own_weights, axis=2)).reshape(cand_total)])
        rounded = lax.optimization_barrier(weights.astype(jnp.bfloat16))
        own_rounded = lax.optimization_barrier(own_weights.astype(jnp.bfloat16))
        numerator = jnp.dot(rounded.astype(jnp.float32), src_values)
        own_part = jnp.einsum('cqk,ckd->cqd', own_rounded.astype(jnp.float32), mine_values).reshape(cand_total, HD)
        numerator = numerator + jnp.concatenate([jnp.zeros((SPAN, HD), jnp.float32), own_part], axis=0)
        return (numerator / denominator[:, None]).astype(jnp.bfloat16)
    heads_out = lax.map(one_head, jnp.arange(HQ, dtype=jnp.int32))
    grouped = heads_out.reshape(N_HEAD, QH_DEV, row_count, HD).transpose(0, 2, 1, 3).reshape(N_HEAD, row_count, QH_DEV * HD)
    wo_grouped = wo.reshape(N_HEAD, QH_DEV * HD, D)

    def add_group(running, pieces):
        partial_value = jnp.dot(pieces[0], pieces[1], preferred_element_type=jnp.float32).astype(jnp.bfloat16)
        partial_value = lax.optimization_barrier(partial_value)
        return (running + partial_value.astype(jnp.float32), None)
    summed, _ = lax.scan(add_group, jnp.zeros((row_count, D), jnp.float32), (grouped, wo_grouped))
    cand_valid = (jnp.arange(CLEN, dtype=jnp.int32)[None, :] < cand_len[:, None]).reshape(cand_total)
    row_valid = jnp.concatenate([jnp.ones((SPAN,), bool), cand_valid])
    result = jnp.where(row_valid[:, None], summed, 0.0).astype(jnp.bfloat16)
    return (result[:SPAN], result[SPAN:].reshape(NCAND, CLEN, D))
```

```python
import functools
import math

import jax
import jax.numpy as jnp
from jax import lax
from jax.experimental import pallas as pl
from jax.experimental.pallas import tpu as pltpu
from jax.sharding import PartitionSpec as P

epsilon = 1e-06
rope_base = 1000000.0
NX = 4
NZ = 4
HEADS = 4
HD = 128
SPAN_ROWS = 256
CAND_ROWS = 128
ROWS = SPAN_ROWS + CAND_ROWS
LOG2E = 1.4426950408889634
VMEM = 56 * 1024 * 1024


def move_x(block, step):
    route = []
    for x in range(NX):
        for z in range(NZ):
            route.append((x * NZ + z, (x + step) % NX * NZ + z))
    return lax.ppermute(block, "head", route)


def move_z(block, step):
    route = []
    for x in range(NX):
        for z in range(NZ):
            route.append((x * NZ + z, x * NZ + (z + step) % NZ))
    return lax.ppermute(block, "head", route)


def swap_pair(block):
    return lax.ppermute(block, "head", [(h, h ^ 1) for h in range(NX * NZ)])


def project_kernel(place, *refs):
    blocks = refs[: NX * NZ]
    gain, wq, wkv_t, q_gain, cosine, sine, q_out, kv_out, normed = refs[NX * NZ :]
    width = blocks[0].shape[0]
    features = width * NX * NZ
    total = jnp.zeros((1, ROWS), jnp.float32)
    for block in blocks:
        values = block[...].astype(jnp.float32)
        total = total + jnp.sum(values * values, axis=0, keepdims=True)
    scale = lax.rsqrt(total / features + epsilon)
    for kx in range(NX):
        for kz in range(NZ):
            x = lax.rem(place[0] + NX - kx, NX)
            z = lax.rem(place[1] + NZ - kz, NZ)
            rows = pl.ds(pl.multiple_of((x * NZ + z) * width, width), width)
            values = blocks[kx * NZ + kz][...].astype(jnp.float32)
            normed[rows, :] = (values * scale * gain[rows, :]).astype(jnp.bfloat16)
    kv_out[...] = jnp.dot(
        wkv_t[...], normed[...], preferred_element_type=jnp.float32
    ).astype(jnp.bfloat16)
    queries = lax.dot_general(
        normed[...], wq[...], (((0,), (0,)), ((), ())), preferred_element_type=jnp.float32
    )
    for head in range(HEADS):
        values = queries[:, head * HD : (head + 1) * HD]
        mean_square = jnp.mean(values * values, axis=1, keepdims=True)
        values = values * lax.rsqrt(mean_square + epsilon) * q_gain[...]
        turned = values * cosine[...] + pltpu.roll(values, HD // 2, 1) * sine[...]
        q_out[head] = turned.astype(jnp.bfloat16)


def project(place, blocks, gain, wq, wkv_t, q_gain, cosine, sine):
    vmem = pl.BlockSpec(memory_space=pltpu.VMEM)
    return pl.pallas_call(
        project_kernel,
        in_specs=[pl.BlockSpec(memory_space=pltpu.SMEM)] + [vmem] * (len(blocks) + 6),
        out_specs=[vmem, vmem],
        out_shape=[
            jax.ShapeDtypeStruct((HEADS, ROWS, HD), jnp.bfloat16),
            jax.ShapeDtypeStruct((wkv_t.shape[0], ROWS), jnp.bfloat16),
        ],
        scratch_shapes=[pltpu.VMEM((wq.shape[0], ROWS), jnp.bfloat16)],
        compiler_params=pltpu.CompilerParams(vmem_limit_bytes=VMEM),
        cost_estimate=pl.CostEstimate(
            flops=2 * ROWS * 5120 * 640, bytes_accessed=12_000_000, transcendentals=0
        ),
    )(place, *blocks, gain, wq, wkv_t, q_gain, cosine, sine)


def fold(q, keys, values, top, total, keep):
    scores = jnp.dot(q, keys, preferred_element_type=jnp.float32) * (LOG2E / math.sqrt(HD))
    if keep is not None:
        scores = jnp.where(keep, scores, -1e30)
    new_top = jnp.maximum(top, jnp.max(scores, axis=1, keepdims=True))
    factor = jnp.exp2(top - new_top)
    weights = jnp.exp2(scores - new_top[:, :1]).astype(jnp.bfloat16)
    added = lax.dot_general(
        weights, values, (((1,), (1,)), ((), ())), preferred_element_type=jnp.float32
    )
    return new_top, total * jnp.concatenate([factor, factor], axis=1) + added


def with_ones(values):
    return jnp.concatenate([values, jnp.ones_like(values)], axis=0)


def cache_kernel(offset, q, kv, top_out, total_out):
    step = pl.program_id(0)
    count = kv.shape[0]
    width = kv.shape[2]

    @pl.when(step == 0)
    def _():
        top_out[...] = jnp.full(top_out.shape, -1e30, jnp.float32)
        total_out[...] = jnp.zeros(total_out.shape, jnp.float32)

    def run(masked):
        keys = jnp.concatenate([kv[i, :HD, :] for i in range(count)], axis=1)
        values = with_ones(jnp.concatenate([kv[i, HD:, :] for i in range(count)], axis=1))
        keep = None
        if masked:
            slot = lax.broadcasted_iota(jnp.int32, (ROWS, count * width), 1)
            keep = slot + step * (count * width) < offset[0]
        for head in range(HEADS):
            top_out[head], total_out[head] = fold(
                q[head], keys, values, top_out[head], total_out[head], keep
            )

    full = (step + 1) * (count * width) <= offset[0]
    pl.when(full)(lambda: run(False))
    pl.when(jnp.logical_not(full))(lambda: run(True))


def attend_cache(offset, q, kv, per_step):
    steps = kv.shape[0] // per_step
    whole = lambda i: (0, 0, 0)
    return pl.pallas_call(
        cache_kernel,
        grid=(steps,),
        in_specs=[
            pl.BlockSpec(memory_space=pltpu.SMEM),
            pl.BlockSpec(q.shape, whole),
            pl.BlockSpec((per_step,) + kv.shape[1:], lambda i: (i, 0, 0)),
        ],
        out_specs=[
            pl.BlockSpec((HEADS, ROWS, HD), whole),
            pl.BlockSpec((HEADS, ROWS, 2 * HD), whole),
        ],
        out_shape=[
            jax.ShapeDtypeStruct((HEADS, ROWS, HD), jnp.float32),
            jax.ShapeDtypeStruct((HEADS, ROWS, 2 * HD), jnp.float32),
        ],
        compiler_params=pltpu.CompilerParams(vmem_limit_bytes=VMEM),
        cost_estimate=pl.CostEstimate(
            flops=4 * HEADS * ROWS * HD * 8192, bytes_accessed=8_000_000, transcendentals=HEADS * ROWS * 8192
        ),
    )(offset, q, kv)


def span_kernel(place, q, kv, own, top_in, total_in, out, top_ref, total_ref):
    step = pl.program_id(0)
    count = kv.shape[0]
    width = kv.shape[2]
    mine = place[0]

    @pl.when(step == 0)
    def _():
        top_ref[...] = top_in[...]
        total_ref[...] = total_in[...]

    def joined():
        keys = jnp.concatenate([kv[i, :HD, :] for i in range(count)], axis=1)
        values = with_ones(jnp.concatenate([kv[i, HD:, :] for i in range(count)], axis=1))
        return keys, values

    def run(masked):
        keys, values = joined()
        keep = None
        if masked:
            row = lax.broadcasted_iota(jnp.int32, (ROWS, count * width), 0)
            slot = lax.broadcasted_iota(jnp.int32, (ROWS, count * width), 1)
            keep = (row >= SPAN_ROWS) | (slot + step * (count * width) <= row + mine * SPAN_ROWS)
        for head in range(HEADS):
            top_ref[head], total_ref[head] = fold(
                q[head], keys, values, top_ref[head], total_ref[head], keep
            )

    def run_cand():
        keys, values = joined()
        for head in range(HEADS):
            top_ref[head, SPAN_ROWS:], total_ref[head, SPAN_ROWS:] = fold(
                q[head, SPAN_ROWS:], keys, values, top_ref[head, SPAN_ROWS:],
                total_ref[head, SPAN_ROWS:], None,
            )

    full = step * count + count - 1 < mine
    none = step * count > mine
    pl.when(full)(lambda: run(False))
    pl.when(none)(run_cand)
    pl.when(jnp.logical_not(full | none))(lambda: run(True))

    @pl.when(step == pl.num_programs(0) - 1)
    def _():
        values = with_ones(own[HD:, :])
        row = lax.broadcasted_iota(jnp.int32, (CAND_ROWS, CAND_ROWS), 0)
        slot = lax.broadcasted_iota(jnp.int32, (CAND_ROWS, CAND_ROWS), 1)
        for head in range(HEADS):
            _, total = fold(
                q[head, SPAN_ROWS:], own[:HD, :], values, top_ref[head, SPAN_ROWS:],
                total_ref[head, SPAN_ROWS:], slot <= row,
            )
            total = jnp.concatenate([total_ref[head, :SPAN_ROWS], total], axis=0)
            attended = total[:, :HD] / total[:, HD:]
            out[head * HD : (head + 1) * HD, :] = attended.T.astype(jnp.bfloat16)


def attend_span(place, q, kv, own, top, total, per_step):
    steps = kv.shape[0] // per_step
    whole = lambda i: (0, 0, 0)
    flat = lambda i: (0, 0)
    return pl.pallas_call(
        span_kernel,
        grid=(steps,),
        in_specs=[
            pl.BlockSpec(memory_space=pltpu.SMEM),
            pl.BlockSpec(q.shape, whole),
            pl.BlockSpec((per_step,) + kv.shape[1:], lambda i: (i, 0, 0)),
            pl.BlockSpec(own.shape, flat),
            pl.BlockSpec(top.shape, whole),
            pl.BlockSpec(total.shape, whole),
        ],
        out_specs=pl.BlockSpec((HEADS * HD, ROWS), flat),
        out_shape=jax.ShapeDtypeStruct((HEADS * HD, ROWS), jnp.bfloat16),
        scratch_shapes=[
            pltpu.VMEM(top.shape, jnp.float32),
            pltpu.VMEM(total.shape, jnp.float32),
        ],
        compiler_params=pltpu.CompilerParams(vmem_limit_bytes=VMEM),
        cost_estimate=pl.CostEstimate(
            flops=4 * HEADS * ROWS * HD * 4096, bytes_accessed=8_000_000, transcendentals=HEADS * ROWS * 4096
        ),
    )(place, q, kv, own, top, total)


def join_pair(mine, other, parity):
    half = mine.shape[0] // 2
    low = jnp.where(parity == 0, mine, other)
    high = jnp.where(parity == 0, other, mine)
    return jnp.concatenate([low[:half], high[:half], low[half:], high[half:]], axis=0)


def per_device(
    span_x, cand_x, cand_len, offset, norm_gain, wq, wk, wv, q_gain, k_gain, wo, cache_k, cache_v
):
    head = lax.axis_index("head")
    seq = lax.axis_index("seq").astype(jnp.int32)
    at_x, at_z = head // NZ, head % NZ
    parity = head % 2
    width = span_x.shape[1]
    half = HD // 2

    own_x = jnp.concatenate([span_x.T, cand_x[0].T], axis=1)
    blocks = [[None] * NZ for _ in range(NX)]
    blocks[0][0] = own_x
    for kz in (2, 1, 3):
        blocks[0][kz] = move_z(own_x, kz)
    for kx in (2, 1, 3):
        blocks[kx][0] = move_x(own_x, kx)
    for kz in (1, 3):
        blocks[2][kz] = move_z(blocks[2][0], kz)
    for kz in (1, 3, 2):
        for kx in (1, 3, 2):
            if blocks[kx][kz] is None:
                blocks[kx][kz] = move_x(blocks[0][kz], kx)

    cache_half = jnp.concatenate([cache_k.T, cache_v.T], axis=0)
    cache_block = join_pair(cache_half, swap_pair(cache_half), parity)
    cache_all = lax.all_gather(cache_block, "seq")

    start = offset[0]
    span_positions = start + seq * SPAN_ROWS + jnp.arange(SPAN_ROWS, dtype=jnp.int32)
    cand_positions = start + SPAN_ROWS * lax.axis_size("seq") + jnp.arange(CAND_ROWS, dtype=jnp.int32)
    positions = jnp.concatenate([span_positions, cand_positions]).astype(jnp.float32)
    frequency = rope_base ** (-(jnp.arange(half, dtype=jnp.float32) * 2.0 / HD))
    angles = frequency[:, None] * positions[None, :]
    cosine, sine = jnp.cos(angles), jnp.sin(angles)
    q_cosine = jnp.concatenate([cosine, cosine], axis=0).T
    q_sine = jnp.concatenate([-sine, sine], axis=0).T

    place = jnp.stack([at_x, at_z]).astype(jnp.int32)
    wkv_t = jnp.concatenate([wk.T, wv.T], axis=0)
    q, kv_half = project(
        place, [b for row in blocks for b in row], norm_gain[:, None], wq, wkv_t,
        q_gain[None, :], q_cosine, q_sine,
    )

    kv_new = join_pair(kv_half, swap_pair(kv_half), parity)
    raw = kv_new[:HD].astype(jnp.float32)
    raw = raw * lax.rsqrt(jnp.mean(raw * raw, axis=0, keepdims=True) + epsilon) * k_gain[:, None]
    front, back = raw[:half], raw[half:]
    new_keys = jnp.concatenate(
        [front * cosine - back * sine, back * cosine + front * sine], axis=0
    ).astype(jnp.bfloat16)
    new_block = jnp.concatenate([new_keys, kv_new[HD:]], axis=0)
    span_all = lax.all_gather(new_block[:, :SPAN_ROWS], "seq")
    own_block = new_block[:, SPAN_ROWS:]

    top, total = attend_cache(offset, q, cache_all, 2)
    attended = attend_span(seq[None], q, span_all, own_block, top, total, 4)

    wo_t = wo.T
    quarter = NZ * width
    terms = []
    for kx in range(NX):
        rows = (at_x + kx) % NX * quarter
        part = lax.dynamic_slice(wo_t, (rows, 0), (quarter, wo.shape[0]))
        terms.append(
            jnp.dot(part, attended, preferred_element_type=jnp.float32).astype(jnp.bfloat16)
        )
    summed = terms[0].astype(jnp.float32)
    for kx in (2, 1, 3):
        summed = summed + move_x(terms[kx], kx).astype(jnp.float32)
    summed = summed.astype(jnp.bfloat16)
    pieces = [
        lax.dynamic_slice(summed, ((at_z + kz) % NZ * width, 0), (width, ROWS))
        for kz in range(NZ)
    ]
    result = pieces[0].astype(jnp.float32)
    for kz in (2, 1, 3):
        result = result + move_z(pieces[kz], kz).astype(jnp.float32)
    span_out = result[:, :SPAN_ROWS].astype(jnp.bfloat16).T
    valid = jnp.arange(CAND_ROWS, dtype=jnp.int32)[None, :] < cand_len[0]
    cand_out = jnp.where(valid, result[:, SPAN_ROWS:], 0.0).astype(jnp.bfloat16).T[None]
    return span_out, cand_out


def solution(mesh):
    in_specs = (
        P("seq", "head"),
        P("seq", None, "head"),
        P("seq"),
        P(),
        P(),
        P(None, "head"),
        P(None, "head"),
        P(None, "head"),
        P(),
        P(),
        P("head", None),
        P("seq", "head"),
        P("seq", "head"),
    )
    out_specs = (P("seq", "head"), P("seq", None, "head"))
    return jax.shard_map(
        per_device, mesh=mesh, in_specs=in_specs, out_specs=out_specs, check_vma=False
    )
```

```python
import functools
import math

import jax
import jax.numpy as jnp
from jax import lax
from jax.experimental import pallas as pl
from jax.experimental.pallas import tpu as pltpu
from jax.sharding import PartitionSpec as P

epsilon = 1e-06
rope_base = 1000000.0
NX = 4
NZ = 4
HEADS = 4
HD = 128
SPAN_ROWS = 256
CAND_ROWS = 128
ROWS = SPAN_ROWS + CAND_ROWS
LOG2E = 1.4426950408889634
NY = 4
MIB = 1024 * 1024


def move_x(block, step):
    route = []
    for x in range(NX):
        for z in range(NZ):
            route.append((x * NZ + z, (x + step) % NX * NZ + z))
    return lax.ppermute(block, "head", route)


def move_z(block, step):
    route = []
    for x in range(NX):
        for z in range(NZ):
            route.append((x * NZ + z, x * NZ + (z + step) % NZ))
    return lax.ppermute(block, "head", route)


def swap_pair(block):
    return lax.ppermute(block, "head", [(h, h ^ 1) for h in range(NX * NZ)])


def move_y(block, step):
    return lax.ppermute(block, "seq", [(s, (s + 4 * step) % (4 * NY)) for s in range(4 * NY)])


def swap_near(block):
    return lax.ppermute(block, "seq", [(s, s ^ 2) for s in range(4 * NY)])


def swap_core(block):
    return lax.ppermute(block, "seq", [(s, s ^ 1) for s in range(4 * NY)])


def gather_seq(block):
    near = jnp.stack([block, swap_near(block)])
    others = [move_y(near, step) for step in (2, 1, 3)]
    mine = jnp.stack([near, others[1], others[0], others[2]])
    return mine, swap_core(mine)


def after(value, *earlier):
    return lax.optimization_barrier((value,) + earlier)[0]


def whole_spec():
    return pl.BlockSpec(memory_space=pltpu.VMEM)


def project_kernel(layout, place, *refs):
    count = len({ref for ref, _ in layout.values()})
    blocks = refs[:count]
    gain, wq, wkv_t, q_gain, cosine, sine, q_out, kv_out, normed = refs[count:]
    features = gain.shape[0]
    width = features // (NX * NZ)
    total = jnp.zeros((1, ROWS), jnp.float32)
    for block in blocks:
        values = block[...].astype(jnp.float32)
        total = total + jnp.sum(values * values, axis=0, keepdims=True)
    scale = lax.rsqrt(total / features + epsilon)
    for (kx, kz), (ref, part) in layout.items():
        x = lax.rem(place[0] + NX - kx, NX)
        z = lax.rem(place[1] + NZ - kz, NZ)
        rows = pl.ds(pl.multiple_of((x * NZ + z) * width, width), width)
        values = blocks[ref][part * width : (part + 1) * width, :].astype(jnp.float32)
        normed[rows, :] = (values * scale * gain[rows, :]).astype(jnp.bfloat16)
    kv_out[...] = jnp.dot(
        wkv_t[...], normed[...], preferred_element_type=jnp.float32
    ).astype(jnp.bfloat16)
    queries = lax.dot_general(
        normed[...], wq[...], (((0,), (0,)), ((), ())), preferred_element_type=jnp.float32
    )
    for head in range(HEADS):
        values = queries[:, head * HD : (head + 1) * HD]
        mean_square = jnp.mean(values * values, axis=1, keepdims=True)
        values = values * lax.rsqrt(mean_square + epsilon) * q_gain[...]
        turned = values * cosine[...] + pltpu.roll(values, HD // 2, 1) * sine[...]
        q_out[head] = turned.astype(jnp.bfloat16)


def project(layout, place, blocks, gain, wq, wkv_t, q_gain, cosine, sine):
    vmem = whole_spec()
    return pl.pallas_call(
        functools.partial(project_kernel, layout),
        in_specs=[pl.BlockSpec(memory_space=pltpu.SMEM)] + [vmem] * (len(blocks) + 6),
        out_specs=[vmem, vmem],
        out_shape=[
            jax.ShapeDtypeStruct((HEADS, ROWS, HD), jnp.bfloat16),
            jax.ShapeDtypeStruct((wkv_t.shape[0], ROWS), jnp.bfloat16),
        ],
        scratch_shapes=[pltpu.VMEM((wq.shape[0], ROWS), jnp.bfloat16)],
        compiler_params=pltpu.CompilerParams(vmem_limit_bytes=30 * MIB),
        cost_estimate=pl.CostEstimate(
            flops=2 * ROWS * 5120 * 640, bytes_accessed=12_000_000, transcendentals=0
        ),
    )(place, *blocks, gain, wq, wkv_t, q_gain, cosine, sine)


def fold_all(units, keys, values, top, total, keep):
    scale = LOG2E / math.sqrt(HD)
    ready = jnp.dot(units[0][2], keys, preferred_element_type=jnp.float32)
    for index, (head, rows, _) in enumerate(units):
        scores = ready * scale
        if index + 1 < len(units):
            ready = jnp.dot(units[index + 1][2], keys, preferred_element_type=jnp.float32)
        if keep is not None:
            scores = jnp.where(keep, scores, -1e30)
        old_top = top[head, rows]
        new_top = jnp.maximum(old_top, jnp.max(scores, axis=1, keepdims=True))
        factor = jnp.exp2(old_top - new_top)
        weights = jnp.exp2(scores - new_top[:, :1]).astype(jnp.bfloat16)
        added = lax.dot_general(
            weights, values, (((1,), (1,)), ((), ())), preferred_element_type=jnp.float32
        )
        total[head, rows] = total[head, rows] * jnp.concatenate([factor, factor], axis=1) + added
        top[head, rows] = new_top


def whole_units(q):
    return [(head, slice(0, ROWS), q[head]) for head in range(HEADS)]


def side_by_side(kv, low, high):
    return jnp.concatenate([kv[i, low:high, :] for i in range(kv.shape[0])], axis=1)


def cache_kernel(first, limits, q, kv, *refs):
    top, total = refs[-2:]
    if first is None:
        top[...] = jnp.full(top.shape, -1e30, jnp.float32)
        total[...] = jnp.zeros(total.shape, jnp.float32)
        first = 0
    else:
        top[...] = refs[0][...]
        total[...] = refs[1][...]
    count, _, width = kv.shape
    slot = lax.broadcasted_iota(jnp.int32, (HD, width), 1)
    counted = jnp.concatenate(
        [(slot < limits[first + i]).astype(jnp.bfloat16) for i in range(count)], axis=1
    )
    values = jnp.concatenate([side_by_side(kv, HD, 2 * HD), counted], axis=0)
    fold_all(whole_units(q), side_by_side(kv, 0, HD), values, top, total, None)


STATE = [
    jax.ShapeDtypeStruct((HEADS, ROWS, HD), jnp.float32),
    jax.ShapeDtypeStruct((HEADS, ROWS, 2 * HD), jnp.float32),
]


def whole_block(shape):
    return pl.BlockSpec(shape, lambda i: (0,) * len(shape))


def attend_cache(limits, q, kv, part, state):
    count = kv.shape[0] // 2
    state_specs = [whole_block(s.shape) for s in STATE]
    return pl.pallas_call(
        functools.partial(cache_kernel, None if state is None else part * count),
        grid=(1,),
        in_specs=[
            pl.BlockSpec(memory_space=pltpu.SMEM),
            whole_block(q.shape),
            pl.BlockSpec((count,) + kv.shape[1:], lambda i: (part, 0, 0)),
        ] + ([] if state is None else state_specs),
        out_specs=state_specs,
        out_shape=STATE,
        compiler_params=pltpu.CompilerParams(vmem_limit_bytes=28 * MIB),
        cost_estimate=pl.CostEstimate(
            flops=4 * HEADS * ROWS * HD * 2048, bytes_accessed=5_000_000, transcendentals=HEADS * ROWS * 2048
        ),
    )(limits, q, kv, *([] if state is None else state))


def span_kernel(last, ahead, q, kv, *refs):
    top, total = refs[-2:]
    offset = 1 if last else 0
    top[...] = refs[offset][...]
    total[...] = refs[offset + 1][...]
    count, _, width = kv.shape
    row = lax.broadcasted_iota(jnp.int32, (ROWS, width), 0)
    slot = lax.broadcasted_iota(jnp.int32, (ROWS, width), 1)
    beyond = jnp.where(row >= SPAN_ROWS, -(1 << 24), slot - row)
    keep = jnp.concatenate([beyond <= ahead[i] for i in range(count)], axis=1)
    values = side_by_side(kv, HD, 2 * HD)
    values = jnp.concatenate([values, jnp.ones_like(values)], axis=0)
    fold_all(whole_units(q), side_by_side(kv, 0, HD), values, top, total, keep)
    if last:
        own, out = refs[0], refs[3]
        row = lax.broadcasted_iota(jnp.int32, (CAND_ROWS, CAND_ROWS), 0)
        slot = lax.broadcasted_iota(jnp.int32, (CAND_ROWS, CAND_ROWS), 1)
        values = own[HD:, :]
        values = jnp.concatenate([values, jnp.ones_like(values)], axis=0)
        units = [(h, slice(SPAN_ROWS, ROWS), q[h, SPAN_ROWS:]) for h in range(HEADS)]
        fold_all(units, own[:HD, :], values, top, total, slot <= row)
        for head in range(HEADS):
            attended = total[head, :, :HD] / total[head, :, HD:]
            out[head * HD : (head + 1) * HD, :] = attended.T.astype(jnp.bfloat16)


def attend_span(ahead, q, kv, own, state):
    last = own is not None
    state_specs = [whole_block(s.shape) for s in STATE]
    if last:
        out_specs = whole_block((HEADS * HD, ROWS))
        out_shape = jax.ShapeDtypeStruct((HEADS * HD, ROWS), jnp.bfloat16)
    else:
        out_specs, out_shape = state_specs, STATE
    return pl.pallas_call(
        functools.partial(span_kernel, last),
        grid=(1,),
        in_specs=[
            pl.BlockSpec(memory_space=pltpu.SMEM),
            whole_block(q.shape),
            whole_block(kv.shape),
        ] + ([whole_block(own.shape)] if last else []) + state_specs,
        out_specs=out_specs,
        out_shape=out_shape,
        scratch_shapes=[pltpu.VMEM(s.shape, s.dtype) for s in STATE] if last else [],
        compiler_params=pltpu.CompilerParams(vmem_limit_bytes=32 * MIB),
        cost_estimate=pl.CostEstimate(
            flops=4 * HEADS * ROWS * HD * 2048, bytes_accessed=5_000_000, transcendentals=HEADS * ROWS * 2048
        ),
    )(ahead, q, kv, *([own] if last else []), *state)


def output_kernel(picks, *refs):
    attended, (near, far), outs = refs[:NX], refs[NX : NX + 2], refs[NX + 2 :]
    for kz in range(NZ):
        ky = picks[kz]
        total = None
        for kx in range(NX):
            rows = jnp.concatenate(
                [half[ky, i, kx] for half in (near, far) for i in range(2)], axis=0
            )
            term = jnp.dot(rows, attended[kx][...], preferred_element_type=jnp.float32)
            total = term if total is None else total + term
        outs[kz][...] = total.astype(outs[kz].dtype)


def project_out(picks, attended, near, far):
    width = 4 * near.shape[3]
    return pl.pallas_call(
        output_kernel,
        in_specs=[pl.BlockSpec(memory_space=pltpu.SMEM)] + [whole_spec()] * (NX + 2),
        out_specs=[whole_spec()] * NZ,
        out_shape=[
            jax.ShapeDtypeStruct((width, ROWS), jnp.bfloat16 if kz else jnp.float32)
            for kz in range(NZ)
        ],
        compiler_params=pltpu.CompilerParams(vmem_limit_bytes=20 * MIB),
        cost_estimate=pl.CostEstimate(
            flops=2 * ROWS * 2048 * 1280, bytes_accessed=8_000_000, transcendentals=0
        ),
    )(picks, *attended, near, far)


def join_pair(mine, other, parity):
    half = mine.shape[0] // 2
    low = jnp.where(parity == 0, mine, other)
    high = jnp.where(parity == 0, other, mine)
    return jnp.concatenate([low[:half], high[:half], low[half:], high[half:]], axis=0)


def per_device(
    span_x, cand_x, cand_len, offset, norm_gain, wq, wk, wv, q_gain, k_gain, wo, cache_k, cache_v
):
    head = lax.axis_index("head").astype(jnp.int32)
    seq = lax.axis_index("seq").astype(jnp.int32)
    at_x, at_z = head // NZ, head % NZ
    at_y, at_near, at_core = seq // 4, seq // 2 % 2, seq % 2
    parity = head % 2
    width = span_x.shape[1]
    half = HD // 2
    start = offset[0]

    own_x = jnp.concatenate([span_x.T, cand_x[0].T], axis=1)
    z1, z3 = move_z(own_x, 1), move_z(own_x, 3)
    z2 = move_z(own_x, 2)
    x2, x1, x3 = move_x(own_x, 2), move_x(own_x, 1), move_x(own_x, 3)
    pair = jnp.concatenate([z1, z3], axis=0)
    x1_pair, x3_pair = move_x(pair, 1), move_x(pair, 3)
    x2_z1, x2_z3 = move_z(x2, 1), move_z(x2, 3)
    x1_z2, x3_z2, x2_z2 = move_x(z2, 1), move_x(z2, 3), move_x(z2, 2)
    blocks = [own_x, z1, z3, z2, x2, x1, x3, x1_pair, x3_pair, x2_z1, x2_z3, x1_z2, x3_z2, x2_z2]
    layout = {
        (0, 0): (0, 0), (0, 1): (1, 0), (0, 3): (2, 0), (0, 2): (3, 0),
        (2, 0): (4, 0), (1, 0): (5, 0), (3, 0): (6, 0),
        (1, 1): (7, 0), (1, 3): (7, 1), (3, 1): (8, 0), (3, 3): (8, 1),
        (2, 1): (9, 0), (2, 3): (10, 0), (1, 2): (11, 0), (3, 2): (12, 0), (2, 2): (13, 0),
    }

    cache_rows = cache_k.shape[0]
    seen = (seq * cache_rows + jnp.arange(cache_rows, dtype=jnp.int32) < start)[None, :]
    keys_t, values_t = cache_k.T, cache_v.T
    cache_half = jnp.concatenate(
        [jnp.where(seen, keys_t, keys_t[:, :1]), jnp.where(seen, values_t, 0)], axis=0
    )
    cache_half = after(cache_half, own_x)
    cache_block = join_pair(cache_half, swap_pair(cache_half), parity)
    cache_near, cache_far = gather_seq(cache_block)
    cache_near = cache_near.reshape(2 * NY, 2 * HD, cache_rows)
    cache_far = cache_far.reshape(2 * NY, 2 * HD, cache_rows)

    part = width // 4
    shares = [
        lax.dynamic_slice(
            wo, (0, ((at_x + kx) % NX * NZ * 4 + seq) * part), (wo.shape[0], part)
        ).T
        for kx in range(NX)
    ]
    shares = after(tuple(shares), z1, z3)
    wo_block = jnp.stack([shares[0]] + [move_x(shares[kx], kx) for kx in range(1, NX)])
    wo_near, wo_far = gather_seq(wo_block)

    span_positions = start + seq * SPAN_ROWS + jnp.arange(SPAN_ROWS, dtype=jnp.int32)
    cand_positions = start + SPAN_ROWS * 4 * NY + jnp.arange(CAND_ROWS, dtype=jnp.int32)
    positions = jnp.concatenate([span_positions, cand_positions]).astype(jnp.float32)
    frequency = rope_base ** (-(jnp.arange(half, dtype=jnp.float32) * 2.0 / HD))
    angles = frequency[:, None] * positions[None, :]
    cosine, sine = jnp.cos(angles), jnp.sin(angles)
    q_cosine = jnp.concatenate([cosine, cosine], axis=0).T
    q_sine = jnp.concatenate([-sine, sine], axis=0).T

    place = jnp.stack([at_x, at_z])
    wkv_t = jnp.concatenate([wk.T, wv.T], axis=0)
    q, kv_half = project(
        layout, place, blocks, norm_gain[:, None], wq, wkv_t, q_gain[None, :], q_cosine, q_sine
    )

    kv_new = join_pair(kv_half, swap_pair(kv_half), parity)
    raw = kv_new[:HD].astype(jnp.float32)
    raw = raw * lax.rsqrt(jnp.mean(raw * raw, axis=0, keepdims=True) + epsilon) * k_gain[:, None]
    front, back = raw[:half], raw[half:]
    new_keys = jnp.concatenate(
        [front * cosine - back * sine, back * cosine + front * sine], axis=0
    ).astype(jnp.bfloat16)
    new_block = jnp.concatenate([new_keys, kv_new[HD:]], axis=0)
    span_near, span_far = gather_seq(new_block[:, :SPAN_ROWS])
    span_near = span_near.reshape(2 * NY, 2 * HD, SPAN_ROWS)
    span_far = span_far.reshape(2 * NY, 2 * HD, SPAN_ROWS)
    own_block = new_block[:, SPAN_ROWS:]

    def sources(core):
        return jnp.stack(
            [
                ((at_y + NY - ky) % NY * 2 + (at_near + near) % 2) * 2 + core
                for ky in range(NY)
                for near in range(2)
            ]
        )

    from_near, from_far = sources(at_core), sources(1 - at_core)
    near_limits = start - from_near * cache_rows
    far_limits = start - from_far * cache_rows
    state = attend_cache(near_limits, q, cache_near, 0, None)
    state = attend_cache(near_limits, q, cache_near, 1, state)
    state = attend_cache(far_limits, q, cache_far, 0, state)
    state = attend_cache(far_limits, q, cache_far, 1, state)
    state = attend_span((seq - from_near) * SPAN_ROWS, q, span_near, None, state)
    attended = attend_span((seq - from_far) * SPAN_ROWS, q, span_far, own_block, state)

    a2, a1, a3 = move_x(attended, 2), move_x(attended, 1), move_x(attended, 3)
    picks = jnp.stack([(at_y - at_z - kz + 2 * NZ) % NY for kz in range(NZ)])
    pieces = project_out(picks, [attended, a1, a2, a3], wo_near, wo_far)
    result = pieces[0]
    for kz in (2, 1, 3):
        result = result + move_z(pieces[kz], kz).astype(jnp.float32)
    result = result.reshape(2, 2, part, ROWS)
    result = jnp.where(at_core == 1, result[::-1], result)
    result = jnp.where(at_near == 1, result[:, ::-1], result)
    result = result.transpose(1, 0, 2, 3).reshape(width, ROWS)
    span_out = result[:, :SPAN_ROWS].astype(jnp.bfloat16).T
    valid = jnp.arange(CAND_ROWS, dtype=jnp.int32)[None, :] < cand_len[0]
    cand_out = jnp.where(valid, result[:, SPAN_ROWS:], 0.0).astype(jnp.bfloat16).T[None]
    return span_out, cand_out


def solution(mesh):
    in_specs = (
        P("seq", "head"),
        P("seq", None, "head"),
        P("seq"),
        P(),
        P(),
        P(None, "head"),
        P(None, "head"),
        P(None, "head"),
        P(),
        P(),
        P("head", None),
        P("seq", "head"),
        P("seq", "head"),
    )
    out_specs = (P("seq", "head"), P("seq", None, "head"))
    return jax.shard_map(
        per_device, mesh=mesh, in_specs=in_specs, out_specs=out_specs, check_vma=False
    )
```

```python
import functools
import math

import jax
import jax.numpy as jnp
from jax import lax
from jax.experimental import pallas as pl
from jax.experimental.pallas import tpu as pltpu
from jax.sharding import PartitionSpec as P

epsilon = 1e-06
rope_base = 1000000.0
NX = 4
NZ = 4
HEADS = 4
HD = 128
SPAN_ROWS = 256
CAND_ROWS = 128
ROWS = SPAN_ROWS + CAND_ROWS
LOG2E = 1.4426950408889634
NY = 4
MIB = 1024 * 1024


def move_x(block, step):
    route = []
    for x in range(NX):
        for z in range(NZ):
            route.append((x * NZ + z, (x + step) % NX * NZ + z))
    return lax.ppermute(block, "head", route)


def move_z(block, step):
    route = []
    for x in range(NX):
        for z in range(NZ):
            route.append((x * NZ + z, x * NZ + (z + step) % NZ))
    return lax.ppermute(block, "head", route)


def swap_pair(block):
    return lax.ppermute(block, "head", [(h, h ^ 1) for h in range(NX * NZ)])


def move_y(block, step):
    return lax.ppermute(block, "seq", [(s, (s + 4 * step) % (4 * NY)) for s in range(4 * NY)])


def swap_near(block):
    return lax.ppermute(block, "seq", [(s, s ^ 2) for s in range(4 * NY)])


def swap_core(block):
    return lax.ppermute(block, "seq", [(s, s ^ 1) for s in range(4 * NY)])


def spread_y(near):
    others = [move_y(near, step) for step in (2, 1, 3)]
    return [near, others[1], others[0], others[2]]


def after(values, *earlier):
    return lax.optimization_barrier((values, earlier))[0]


def whole_spec():
    return pl.BlockSpec(memory_space=pltpu.VMEM)


def project_kernel(layout, place, *refs):
    count = len({ref for ref, _ in layout.values()})
    blocks = refs[:count]
    gain, wq, wkv_t, q_gain, cosine, sine, q_out, kv_out, normed = refs[count:]
    features = gain.shape[0]
    width = features // (NX * NZ)
    total = jnp.zeros((1, ROWS), jnp.float32)
    for block in blocks:
        values = block[:, :ROWS].astype(jnp.float32)
        total = total + jnp.sum(values * values, axis=0, keepdims=True)
    scale = lax.rsqrt(total / features + epsilon)
    for (kx, kz), (ref, part) in layout.items():
        x = lax.rem(place[0] + NX - kx, NX)
        z = lax.rem(place[1] + NZ - kz, NZ)
        rows = pl.ds(pl.multiple_of((x * NZ + z) * width, width), width)
        values = blocks[ref][part * width : (part + 1) * width, :ROWS].astype(jnp.float32)
        normed[rows, :] = (values * scale * gain[rows, :]).astype(jnp.bfloat16)
    kv_out[...] = jnp.dot(
        wkv_t[...], normed[...], preferred_element_type=jnp.float32
    ).astype(jnp.bfloat16)
    queries = lax.dot_general(
        normed[...], wq[...], (((0,), (0,)), ((), ())), preferred_element_type=jnp.float32
    )
    for head in range(HEADS):
        values = queries[:, head * HD : (head + 1) * HD]
        mean_square = jnp.mean(values * values, axis=1, keepdims=True)
        values = values * lax.rsqrt(mean_square + epsilon) * q_gain[...]
        turned = values * cosine[...] + pltpu.roll(values, HD // 2, 1) * sine[...]
        q_out[head] = turned.astype(jnp.bfloat16)


def project(layout, place, blocks, gain, wq, wkv_t, q_gain, cosine, sine):
    vmem = whole_spec()
    return pl.pallas_call(
        functools.partial(project_kernel, layout),
        in_specs=[pl.BlockSpec(memory_space=pltpu.SMEM)] + [vmem] * (len(blocks) + 6),
        out_specs=[vmem, vmem],
        out_shape=[
            jax.ShapeDtypeStruct((HEADS, ROWS, HD), jnp.bfloat16),
            jax.ShapeDtypeStruct((wkv_t.shape[0], ROWS), jnp.bfloat16),
        ],
        scratch_shapes=[pltpu.VMEM((wq.shape[0], ROWS), jnp.bfloat16)],
        compiler_params=pltpu.CompilerParams(vmem_limit_bytes=30 * MIB),
        cost_estimate=pl.CostEstimate(
            flops=2 * ROWS * 5120 * 640, bytes_accessed=12_000_000, transcendentals=0
        ),
    )(place, *blocks, gain, wq, wkv_t, q_gain, cosine, sine)


def fold_all(units, keys, values, top, total, keep):
    scale = LOG2E / math.sqrt(HD)
    ready = jnp.dot(units[0][2], keys, preferred_element_type=jnp.float32)
    for index, (head, rows, _) in enumerate(units):
        scores = ready * scale
        if index + 1 < len(units):
            ready = jnp.dot(units[index + 1][2], keys, preferred_element_type=jnp.float32)
        if keep is not None:
            scores = jnp.where(keep, scores, -1e30)
        old_top = top[head, rows]
        new_top = jnp.maximum(old_top, jnp.max(scores, axis=1, keepdims=True))
        factor = jnp.exp2(old_top - new_top)
        weights = jnp.exp2(scores - new_top[:, :1]).astype(jnp.bfloat16)
        added = lax.dot_general(
            weights, values, (((1,), (1,)), ((), ())), preferred_element_type=jnp.float32
        )
        total[head, rows] = total[head, rows] * jnp.concatenate([factor, factor], axis=1) + added
        top[head, rows] = new_top


def whole_units(q):
    return [(head, slice(0, ROWS), q[head]) for head in range(HEADS)]


def side_by_side(kv, low, high):
    return jnp.concatenate([kv[i, low:high, :] for i in range(kv.shape[0])], axis=1)


def cache_kernel(first, limits, q, kv, *refs):
    top, total = refs[-2:]
    if first is None:
        top[...] = jnp.full(top.shape, -1e30, jnp.float32)
        total[...] = jnp.zeros(total.shape, jnp.float32)
        first = 0
    else:
        top[...] = refs[0][...]
        total[...] = refs[1][...]
    count, _, width = kv.shape
    slot = lax.broadcasted_iota(jnp.int32, (HD, width), 1)
    counted = jnp.concatenate(
        [(slot < limits[first + i]).astype(jnp.bfloat16) for i in range(count)], axis=1
    )
    values = jnp.concatenate([side_by_side(kv, HD, 2 * HD), counted], axis=0)
    fold_all(whole_units(q), side_by_side(kv, 0, HD), values, top, total, None)


STATE = [
    jax.ShapeDtypeStruct((HEADS, ROWS, HD), jnp.float32),
    jax.ShapeDtypeStruct((HEADS, ROWS, 2 * HD), jnp.float32),
]


def whole_block(shape):
    return pl.BlockSpec(shape, lambda i: (0,) * len(shape))


def attend_cache(limits, q, kv, part, state):
    count = kv.shape[0] // 2
    state_specs = [whole_block(s.shape) for s in STATE]
    return pl.pallas_call(
        functools.partial(cache_kernel, None if state is None else part * count),
        grid=(1,),
        in_specs=[
            pl.BlockSpec(memory_space=pltpu.SMEM),
            whole_block(q.shape),
            pl.BlockSpec((count,) + kv.shape[1:], lambda i: (part, 0, 0)),
        ] + ([] if state is None else state_specs),
        out_specs=state_specs,
        out_shape=STATE,
        compiler_params=pltpu.CompilerParams(vmem_limit_bytes=28 * MIB),
        cost_estimate=pl.CostEstimate(
            flops=4 * HEADS * ROWS * HD * 2048, bytes_accessed=5_000_000, transcendentals=HEADS * ROWS * 2048
        ),
    )(limits, q, kv, *([] if state is None else state))


def span_kernel(last, ahead, q, kv, *refs):
    top, total = refs[-2:]
    offset = 1 if last else 0
    top[...] = refs[offset][...]
    total[...] = refs[offset + 1][...]
    count, _, width = kv.shape
    row = lax.broadcasted_iota(jnp.int32, (ROWS, width), 0)
    slot = lax.broadcasted_iota(jnp.int32, (ROWS, width), 1)
    beyond = jnp.where(row >= SPAN_ROWS, -(1 << 24), slot - row)
    keep = jnp.concatenate([beyond <= ahead[i] for i in range(count)], axis=1)
    values = side_by_side(kv, HD, 2 * HD)
    values = jnp.concatenate([values, jnp.ones_like(values)], axis=0)
    fold_all(whole_units(q), side_by_side(kv, 0, HD), values, top, total, keep)
    if last:
        own, out = refs[0], refs[3]
        row = lax.broadcasted_iota(jnp.int32, (CAND_ROWS, CAND_ROWS), 0)
        slot = lax.broadcasted_iota(jnp.int32, (CAND_ROWS, CAND_ROWS), 1)
        values = own[HD:, :]
        values = jnp.concatenate([values, jnp.ones_like(values)], axis=0)
        units = [(h, slice(SPAN_ROWS, ROWS), q[h, SPAN_ROWS:]) for h in range(HEADS)]
        fold_all(units, own[:HD, :], values, top, total, slot <= row)
        for head in range(HEADS):
            attended = total[head, :, :HD] / total[head, :, HD:]
            out[head * HD : (head + 1) * HD, :] = attended.T.astype(jnp.bfloat16)


def attend_span(ahead, q, kv, own, state):
    last = own is not None
    state_specs = [whole_block(s.shape) for s in STATE]
    if last:
        out_specs = whole_block((HEADS * HD, ROWS))
        out_shape = jax.ShapeDtypeStruct((HEADS * HD, ROWS), jnp.bfloat16)
    else:
        out_specs, out_shape = state_specs, STATE
    return pl.pallas_call(
        functools.partial(span_kernel, last),
        grid=(1,),
        in_specs=[
            pl.BlockSpec(memory_space=pltpu.SMEM),
            whole_block(q.shape),
            whole_block(kv.shape),
        ] + ([whole_block(own.shape)] if last else []) + state_specs,
        out_specs=out_specs,
        out_shape=out_shape,
        scratch_shapes=[pltpu.VMEM(s.shape, s.dtype) for s in STATE] if last else [],
        compiler_params=pltpu.CompilerParams(vmem_limit_bytes=32 * MIB),
        cost_estimate=pl.CostEstimate(
            flops=4 * HEADS * ROWS * HD * 2048, bytes_accessed=5_000_000, transcendentals=HEADS * ROWS * 2048
        ),
    )(ahead, q, kv, *([own] if last else []), *state)


def output_kernel(picks, *refs):
    attended, (near, far), outs = refs[:NX], refs[NX : NX + 2], refs[NX + 2 :]
    for kz in range(NZ):
        ky = picks[kz]
        total = None
        for kx in range(NX):
            rows = jnp.concatenate(
                [half[ky, i, kx] for half in (near, far) for i in range(2)], axis=0
            )
            term = jnp.dot(rows, attended[kx][...], preferred_element_type=jnp.float32)
            total = term if total is None else total + term
        outs[kz][...] = total.astype(outs[kz].dtype)


def project_out(picks, attended, near, far):
    width = 4 * near.shape[3]
    return pl.pallas_call(
        output_kernel,
        in_specs=[pl.BlockSpec(memory_space=pltpu.SMEM)] + [whole_spec()] * (NX + 2),
        out_specs=[whole_spec()] * NZ,
        out_shape=[
            jax.ShapeDtypeStruct((width, ROWS), jnp.bfloat16 if kz else jnp.float32)
            for kz in range(NZ)
        ],
        compiler_params=pltpu.CompilerParams(vmem_limit_bytes=20 * MIB),
        cost_estimate=pl.CostEstimate(
            flops=2 * ROWS * 2048 * 1280, bytes_accessed=8_000_000, transcendentals=0
        ),
    )(picks, *attended, near, far)


def join_pair(mine, other, parity):
    half = mine.shape[0] // 2
    low = jnp.where(parity == 0, mine, other)
    high = jnp.where(parity == 0, other, mine)
    return jnp.concatenate([low[:half], high[:half], low[half:], high[half:]], axis=0)


def per_device(
    span_x, cand_x, cand_len, offset, norm_gain, wq, wk, wv, q_gain, k_gain, wo, cache_k, cache_v
):
    head = lax.axis_index("head").astype(jnp.int32)
    seq = lax.axis_index("seq").astype(jnp.int32)
    at_x, at_z = head // NZ, head % NZ
    at_y, at_near, at_core = seq // 4, seq // 2 % 2, seq % 2
    parity = head % 2
    width = span_x.shape[1]
    half = HD // 2
    start = offset[0]

    part = width // 4
    own_x = jnp.concatenate([span_x.T, cand_x[0].T], axis=1)
    cache_rows = cache_k.shape[0]
    seen = (seq * cache_rows + jnp.arange(cache_rows, dtype=jnp.int32) < start)[None, :]
    keys_t, values_t = cache_k.T, cache_v.T
    cache_half = jnp.concatenate(
        [jnp.where(seen, keys_t, keys_t[:, :1]), jnp.where(seen, values_t, 0)], axis=0
    )
    z1, z3 = move_z(own_x, 1), move_z(own_x, 3)
    cache_block = join_pair(cache_half, swap_pair(cache_half), parity)
    cache_near = jnp.stack([cache_block, swap_near(cache_block)])
    shares = []
    for kx in range(NX):
        column = ((at_x + kx) % NX * NZ * 4 + seq) * part
        share = lax.dynamic_slice(wo, (0, column), (wo.shape[0], part)).T
        share = share.reshape(part, 4, HD).transpose(1, 0, 2).reshape(width, HD)
        shares.append(jnp.concatenate([own_x, share], axis=1))
    x2, x1, x3 = (move_x(shares[kx], kx) for kx in (2, 1, 3))

    z1, z3, x1, x2, x3, cache_near, own_x = after((z1, z3, x1, x2, x3, cache_near, own_x))
    pair = jnp.concatenate([z1, z3], axis=0)
    x2_pair, x1_pair, x3_pair = move_x(pair, 2), move_x(pair, 1), move_x(pair, 3)
    z2 = move_z(own_x, 2)
    cache_parts = spread_y(cache_near)
    wo_block = jnp.stack(
        [
            b[:, ROWS:].reshape(4, part, HD).transpose(1, 0, 2).reshape(part, 4 * HD)
            for b in (shares[0], x1, x2, x3)
        ]
    )
    wo_near = jnp.stack([wo_block, swap_near(wo_block)])

    z2, x2_pair, x1_pair, x3_pair, wo_near = after((z2, x2_pair, x1_pair, x3_pair, wo_near))
    x2_z2, x1_z2, x3_z2 = move_x(z2, 2), move_x(z2, 1), move_x(z2, 3)
    wo_parts = spread_y(wo_near)
    blocks = [own_x, z1, z3, z2, x1, x2, x3, x1_pair, x2_pair, x3_pair, x1_z2, x2_z2, x3_z2]
    layout = {(0, 0): (0, 0), (0, 1): (1, 0), (0, 3): (2, 0), (0, 2): (3, 0)}
    for kx in range(1, NX):
        layout[kx, 0] = (3 + kx, 0)
        layout[kx, 1], layout[kx, 3] = (6 + kx, 0), (6 + kx, 1)
        layout[kx, 2] = (9 + kx, 0)

    span_positions = start + seq * SPAN_ROWS + jnp.arange(SPAN_ROWS, dtype=jnp.int32)
    cand_positions = start + SPAN_ROWS * 4 * NY + jnp.arange(CAND_ROWS, dtype=jnp.int32)
    positions = jnp.concatenate([span_positions, cand_positions]).astype(jnp.float32)
    frequency = rope_base ** (-(jnp.arange(half, dtype=jnp.float32) * 2.0 / HD))
    angles = frequency[:, None] * positions[None, :]
    cosine, sine = jnp.cos(angles), jnp.sin(angles)
    q_cosine = jnp.concatenate([cosine, cosine], axis=0).T
    q_sine = jnp.concatenate([-sine, sine], axis=0).T

    place = jnp.stack([at_x, at_z])
    wkv_t = jnp.concatenate([wk.T, wv.T], axis=0)
    q, kv_half = project(
        layout, place, blocks, norm_gain[:, None], wq, wkv_t, q_gain[None, :], q_cosine, q_sine
    )

    def sources(core):
        return jnp.stack(
            [
                ((at_y + NY - ky) % NY * 2 + (at_near + near) % 2) * 2 + core
                for ky in range(NY)
                for near in range(2)
            ]
        )

    from_near, from_far = sources(at_core), sources(1 - at_core)
    near_limits = start - from_near * cache_rows
    far_limits = start - from_far * cache_rows
    cache_near = jnp.stack(cache_parts)
    cache_far = swap_core(cache_near)
    cache_shape = (2 * NY, 2 * HD, cache_rows)
    cache_near, cache_far = cache_near.reshape(cache_shape), cache_far.reshape(cache_shape)

    other_half = swap_pair(kv_half)
    state = attend_cache(near_limits, q, cache_near, 0, None)
    kv_new = join_pair(kv_half, other_half, parity)
    raw = kv_new[:HD].astype(jnp.float32)
    raw = raw * lax.rsqrt(jnp.mean(raw * raw, axis=0, keepdims=True) + epsilon) * k_gain[:, None]
    front, back = raw[:half], raw[half:]
    new_keys = jnp.concatenate(
        [front * cosine - back * sine, back * cosine + front * sine], axis=0
    ).astype(jnp.bfloat16)
    new_block = jnp.concatenate([new_keys, kv_new[HD:]], axis=0)
    new_block, state = after((new_block, state))
    span_block, own_block = new_block[:, :SPAN_ROWS], new_block[:, SPAN_ROWS:]
    other_near = swap_near(span_block)
    state = attend_cache(near_limits, q, cache_near, 1, state)
    other_near, state = after((other_near, state))
    span_parts = spread_y(jnp.stack([span_block, other_near]))
    state = attend_cache(far_limits, q, cache_far, 0, state)
    state = attend_cache(far_limits, q, cache_far, 1, state)
    span_parts, wo_parts, state = after((span_parts, wo_parts, state))
    span_near, wo_near = jnp.stack(span_parts), jnp.stack(wo_parts)
    span_far, wo_far = swap_core(span_near), swap_core(wo_near)
    span_shape = (2 * NY, 2 * HD, SPAN_ROWS)
    span_near, span_far = span_near.reshape(span_shape), span_far.reshape(span_shape)
    state = attend_span((seq - from_near) * SPAN_ROWS, q, span_near, None, state)
    attended = attend_span((seq - from_far) * SPAN_ROWS, q, span_far, own_block, state)

    a2, a1, a3 = move_x(attended, 2), move_x(attended, 1), move_x(attended, 3)
    picks = jnp.stack([(at_y - at_z - kz + 2 * NZ) % NY for kz in range(NZ)])
    pieces = project_out(picks, [attended, a1, a2, a3], wo_near, wo_far)
    result = pieces[0]
    for kz in (2, 1, 3):
        result = result + move_z(pieces[kz], kz).astype(jnp.float32)
    result = result.reshape(2, 2, part, ROWS)
    result = jnp.where(at_core == 1, result[::-1], result)
    result = jnp.where(at_near == 1, result[:, ::-1], result)
    result = result.transpose(1, 0, 2, 3).reshape(width, ROWS)
    span_out = result[:, :SPAN_ROWS].astype(jnp.bfloat16).T
    valid = jnp.arange(CAND_ROWS, dtype=jnp.int32)[None, :] < cand_len[0]
    cand_out = jnp.where(valid, result[:, SPAN_ROWS:], 0.0).astype(jnp.bfloat16).T[None]
    return span_out, cand_out


def solution(mesh):
    in_specs = (
        P("seq", "head"),
        P("seq", None, "head"),
        P("seq"),
        P(),
        P(),
        P(None, "head"),
        P(None, "head"),
        P(None, "head"),
        P(),
        P(),
        P("head", None),
        P("seq", "head"),
        P("seq", "head"),
    )
    out_specs = (P("seq", "head"), P("seq", None, "head"))
    return jax.shard_map(
        per_device, mesh=mesh, in_specs=in_specs, out_specs=out_specs, check_vma=False
    )
```

```python
import functools
import math

import jax
import jax.numpy as jnp
from jax import lax
from jax.experimental import pallas as pl
from jax.experimental.pallas import tpu as pltpu
from jax.sharding import PartitionSpec as P

epsilon = 1e-06
rope_base = 1000000.0
NX = 4
NZ = 4
HEADS = 4
HD = 128
SPAN_ROWS = 256
CAND_ROWS = 128
ROWS = SPAN_ROWS + CAND_ROWS
LOG2E = 1.4426950408889634
NY = 4
MIB = 1024 * 1024


def move_x(block, step):
    route = []
    for x in range(NX):
        for z in range(NZ):
            route.append((x * NZ + z, (x + step) % NX * NZ + z))
    return lax.ppermute(block, "head", route)


def move_z(block, step):
    route = []
    for x in range(NX):
        for z in range(NZ):
            route.append((x * NZ + z, x * NZ + (z + step) % NZ))
    return lax.ppermute(block, "head", route)


def swap_pair(block):
    return lax.ppermute(block, "head", [(h, h ^ 1) for h in range(NX * NZ)])


def move_y(block, step):
    return lax.ppermute(block, "seq", [(s, (s + 4 * step) % (4 * NY)) for s in range(4 * NY)])


def swap_near(block):
    return lax.ppermute(block, "seq", [(s, s ^ 2) for s in range(4 * NY)])


def swap_core(block):
    return lax.ppermute(block, "seq", [(s, s ^ 1) for s in range(4 * NY)])


def spread_y(near):
    others = [move_y(near, step) for step in (2, 1, 3)]
    return [near, others[1], others[0], others[2]]


def after(values, *earlier):
    return lax.optimization_barrier((values, earlier))[0]


def whole_spec():
    return pl.BlockSpec(memory_space=pltpu.VMEM)


def project_kernel(layout, place, *refs):
    count = len({ref for ref, _ in layout.values()})
    blocks = refs[:count]
    gain, wq, wkv_t, q_gain, cosine, sine, q_out, kv_out, normed = refs[count:]
    features = gain.shape[0]
    width = features // (NX * NZ)
    total = jnp.zeros((1, ROWS), jnp.float32)
    for block in blocks:
        values = block[:, :ROWS].astype(jnp.float32)
        total = total + jnp.sum(values * values, axis=0, keepdims=True)
    scale = lax.rsqrt(total / features + epsilon)
    for (kx, kz), (ref, part) in layout.items():
        x = lax.rem(place[0] + NX - kx, NX)
        z = lax.rem(place[1] + NZ - kz, NZ)
        rows = pl.ds(pl.multiple_of((x * NZ + z) * width, width), width)
        values = blocks[ref][part * width : (part + 1) * width, :ROWS].astype(jnp.float32)
        normed[rows, :] = (values * scale * gain[rows, :]).astype(jnp.bfloat16)
    kv_out[...] = jnp.dot(
        wkv_t[...], normed[...], preferred_element_type=jnp.float32
    ).astype(jnp.bfloat16)
    queries = lax.dot_general(
        normed[...], wq[...], (((0,), (0,)), ((), ())), preferred_element_type=jnp.float32
    )
    for head in range(HEADS):
        values = queries[:, head * HD : (head + 1) * HD]
        mean_square = jnp.mean(values * values, axis=1, keepdims=True)
        values = values * lax.rsqrt(mean_square + epsilon) * q_gain[...]
        turned = values * cosine[...] + pltpu.roll(values, HD // 2, 1) * sine[...]
        q_out[head] = turned.astype(jnp.bfloat16)


def project(layout, place, blocks, gain, wq, wkv_t, q_gain, cosine, sine):
    vmem = whole_spec()
    return pl.pallas_call(
        functools.partial(project_kernel, layout),
        in_specs=[pl.BlockSpec(memory_space=pltpu.SMEM)] + [vmem] * (len(blocks) + 6),
        out_specs=[vmem, vmem],
        out_shape=[
            jax.ShapeDtypeStruct((HEADS, ROWS, HD), jnp.bfloat16),
            jax.ShapeDtypeStruct((wkv_t.shape[0], ROWS), jnp.bfloat16),
        ],
        scratch_shapes=[pltpu.VMEM((wq.shape[0], ROWS), jnp.bfloat16)],
        compiler_params=pltpu.CompilerParams(vmem_limit_bytes=30 * MIB),
        cost_estimate=pl.CostEstimate(
            flops=2 * ROWS * 5120 * 640, bytes_accessed=12_000_000, transcendentals=0
        ),
    )(place, *blocks, gain, wq, wkv_t, q_gain, cosine, sine)


def fold_all(units, keys, values, top, total, keep):
    scale = LOG2E / math.sqrt(HD)
    ready = jnp.dot(units[0][2], keys, preferred_element_type=jnp.float32)
    for index, (head, rows, _) in enumerate(units):
        scores = ready * scale
        if index + 1 < len(units):
            ready = jnp.dot(units[index + 1][2], keys, preferred_element_type=jnp.float32)
        if keep is not None:
            scores = jnp.where(keep, scores, -1e30)
        old_top = top[head, rows]
        new_top = jnp.maximum(old_top, jnp.max(scores, axis=1, keepdims=True))
        factor = jnp.exp2(old_top - new_top)
        weights = jnp.exp2(scores - new_top[:, :1]).astype(jnp.bfloat16)
        added = lax.dot_general(
            weights, values, (((1,), (1,)), ((), ())), preferred_element_type=jnp.float32
        )
        total[head, rows] = total[head, rows] * jnp.concatenate([factor, factor], axis=1) + added
        top[head, rows] = new_top


def whole_units(q):
    return [(head, slice(0, ROWS), q[head]) for head in range(HEADS)]


def side_by_side(kv, low, high):
    return jnp.concatenate([kv[i, low:high, :] for i in range(kv.shape[0])], axis=1)


def cache_kernel(first, limits, q, kv, *refs):
    top, total = refs[-2:]
    if first is None:
        top[...] = jnp.full(top.shape, -1e30, jnp.float32)
        total[...] = jnp.zeros(total.shape, jnp.float32)
        first = 0
    else:
        top[...] = refs[0][...]
        total[...] = refs[1][...]
    count, _, width = kv.shape
    slot = lax.broadcasted_iota(jnp.int32, (HD, width), 1)
    counted = jnp.concatenate(
        [(slot < limits[first + i]).astype(jnp.bfloat16) for i in range(count)], axis=1
    )
    values = jnp.concatenate([side_by_side(kv, HD, 2 * HD), counted], axis=0)
    fold_all(whole_units(q), side_by_side(kv, 0, HD), values, top, total, None)


STATE = [
    jax.ShapeDtypeStruct((HEADS, ROWS, HD), jnp.float32),
    jax.ShapeDtypeStruct((HEADS, ROWS, 2 * HD), jnp.float32),
]


def whole_block(shape):
    return pl.BlockSpec(shape, lambda i: (0,) * len(shape))


def attend_cache(limits, q, kv, part, state):
    count = kv.shape[0] // 4
    state_specs = [whole_block(s.shape) for s in STATE]
    return pl.pallas_call(
        functools.partial(cache_kernel, None if state is None else part * count),
        grid=(1,),
        in_specs=[
            pl.BlockSpec(memory_space=pltpu.SMEM),
            whole_block(q.shape),
            pl.BlockSpec((count,) + kv.shape[1:], lambda i: (part, 0, 0)),
        ] + ([] if state is None else state_specs),
        out_specs=state_specs,
        out_shape=STATE,
        compiler_params=pltpu.CompilerParams(vmem_limit_bytes=28 * MIB),
        cost_estimate=pl.CostEstimate(
            flops=4 * HEADS * ROWS * HD * 2048, bytes_accessed=5_000_000, transcendentals=HEADS * ROWS * 2048
        ),
    )(limits, q, kv, *([] if state is None else state))


def span_kernel(last, ahead, q, kv, *refs):
    top, total = refs[-2:]
    offset = 1 if last else 0
    top[...] = refs[offset][...]
    total[...] = refs[offset + 1][...]
    count, _, width = kv.shape
    row = lax.broadcasted_iota(jnp.int32, (ROWS, width), 0)
    slot = lax.broadcasted_iota(jnp.int32, (ROWS, width), 1)
    beyond = jnp.where(row >= SPAN_ROWS, -(1 << 24), slot - row)
    keep = jnp.concatenate([beyond <= ahead[i] for i in range(count)], axis=1)
    values = side_by_side(kv, HD, 2 * HD)
    values = jnp.concatenate([values, jnp.ones_like(values)], axis=0)
    fold_all(whole_units(q), side_by_side(kv, 0, HD), values, top, total, keep)
    if last:
        own, out = refs[0], refs[3]
        row = lax.broadcasted_iota(jnp.int32, (CAND_ROWS, CAND_ROWS), 0)
        slot = lax.broadcasted_iota(jnp.int32, (CAND_ROWS, CAND_ROWS), 1)
        values = own[HD:, :]
        values = jnp.concatenate([values, jnp.ones_like(values)], axis=0)
        units = [(h, slice(SPAN_ROWS, ROWS), q[h, SPAN_ROWS:]) for h in range(HEADS)]
        fold_all(units, own[:HD, :], values, top, total, slot <= row)
        for head in range(HEADS):
            attended = total[head, :, :HD] / total[head, :, HD:]
            out[head * HD : (head + 1) * HD, :] = attended.T.astype(jnp.bfloat16)


def attend_span(ahead, q, kv, own, state):
    last = own is not None
    state_specs = [whole_block(s.shape) for s in STATE]
    if last:
        out_specs = whole_block((HEADS * HD, ROWS))
        out_shape = jax.ShapeDtypeStruct((HEADS * HD, ROWS), jnp.bfloat16)
    else:
        out_specs, out_shape = state_specs, STATE
    return pl.pallas_call(
        functools.partial(span_kernel, last),
        grid=(1,),
        in_specs=[
            pl.BlockSpec(memory_space=pltpu.SMEM),
            whole_block(q.shape),
            whole_block(kv.shape),
        ] + ([whole_block(own.shape)] if last else []) + state_specs,
        out_specs=out_specs,
        out_shape=out_shape,
        scratch_shapes=[pltpu.VMEM(s.shape, s.dtype) for s in STATE] if last else [],
        compiler_params=pltpu.CompilerParams(vmem_limit_bytes=32 * MIB),
        cost_estimate=pl.CostEstimate(
            flops=4 * HEADS * ROWS * HD * 2048, bytes_accessed=5_000_000, transcendentals=HEADS * ROWS * 2048
        ),
    )(ahead, q, kv, *([own] if last else []), *state)


def output_kernel(picks, *refs):
    attended, regrouped, outs = refs[:NX], refs[NX], refs[NX + 1 :]
    for kz in range(NZ):
        total = None
        for kx in range(NX):
            rows = jnp.concatenate([regrouped[picks[kz] + i, kx] for i in range(4)], axis=0)
            term = jnp.dot(rows, attended[kx][...], preferred_element_type=jnp.float32)
            total = term if total is None else total + term
        outs[kz][...] = total.astype(outs[kz].dtype)


def project_out(picks, attended, regrouped):
    width = 4 * regrouped.shape[2]
    return pl.pallas_call(
        output_kernel,
        in_specs=[pl.BlockSpec(memory_space=pltpu.SMEM)] + [whole_spec()] * (NX + 1),
        out_specs=[whole_spec()] * NZ,
        out_shape=[
            jax.ShapeDtypeStruct((width, ROWS), jnp.bfloat16 if kz else jnp.float32)
            for kz in range(NZ)
        ],
        compiler_params=pltpu.CompilerParams(vmem_limit_bytes=20 * MIB),
        cost_estimate=pl.CostEstimate(
            flops=2 * ROWS * 2048 * 1280, bytes_accessed=8_000_000, transcendentals=0
        ),
    )(picks, *attended, regrouped)


def join_pair(mine, other, parity):
    half = mine.shape[0] // 2
    low = jnp.where(parity == 0, mine, other)
    high = jnp.where(parity == 0, other, mine)
    return jnp.concatenate([low[:half], high[:half], low[half:], high[half:]], axis=0)


def per_device(
    span_x, cand_x, cand_len, offset, norm_gain, wq, wk, wv, q_gain, k_gain, wo, cache_k, cache_v
):
    head = lax.axis_index("head").astype(jnp.int32)
    seq = lax.axis_index("seq").astype(jnp.int32)
    at_x, at_z = head // NZ, head % NZ
    at_y, at_near, at_core = seq // 4, seq // 2 % 2, seq % 2
    parity = head % 2
    width = span_x.shape[1]
    half = HD // 2
    start = offset[0]

    part = width // 4
    own_x = jnp.concatenate([span_x.T, cand_x[0].T], axis=1)
    cache_rows = cache_k.shape[0]
    seen = (seq * cache_rows + jnp.arange(cache_rows, dtype=jnp.int32) < start)[None, :]
    keys_t, values_t = cache_k.T, cache_v.T
    cache_half = jnp.concatenate(
        [jnp.where(seen, keys_t, keys_t[:, :1]), jnp.where(seen, values_t, 0)], axis=0
    )
    z1, z3, z2 = move_z(own_x, 1), move_z(own_x, 3), move_z(own_x, 2)
    other_cache, z1, z3 = after((swap_pair(cache_half), z1, z3))
    cache_block = join_pair(cache_half, other_cache, parity)
    cache_all = lax.all_gather(cache_block, "seq")
    shares = []
    for kx in range(NX):
        column = ((at_x + kx) % NX * NZ * 4 + seq) * part
        share = lax.dynamic_slice(wo, (0, column), (wo.shape[0], part)).T
        share = share.reshape(part, 4, HD).transpose(1, 0, 2).reshape(width, HD)
        shares.append(jnp.concatenate([own_x, share], axis=1))
    x2, x1, x3 = (move_x(shares[kx], kx) for kx in (2, 1, 3))

    z1, z2, z3, x1, x2, x3 = after((z1, z2, z3, x1, x2, x3))
    stack = jnp.concatenate([z1, z2, z3], axis=0)
    x1_z, x3_z = move_x(stack, 1), move_x(stack, 3)
    x2_z2 = move_x(z2, 2)
    x2_own = x2[:, :ROWS]
    x2_z1, x2_z3 = move_z(x2_own, 1), move_z(x2_own, 3)
    wo_block = jnp.stack(
        [
            b[:, ROWS:].reshape(4, part, HD).transpose(1, 0, 2).reshape(part, 4 * HD)
            for b in (shares[0], x1, x2, x3)
        ]
    )
    blocks = [own_x, z1, z2, z3, x1, x2, x3, x1_z, x3_z, x2_z1, x2_z2, x2_z3]
    layout = {(0, 0): (0, 0), (2, 0): (5, 0), (1, 0): (4, 0), (3, 0): (6, 0)}
    for kz in range(1, NZ):
        layout[0, kz] = (kz, 0)
        layout[1, kz], layout[3, kz] = (7, kz - 1), (8, kz - 1)
        layout[2, kz] = (8 + kz, 0)

    span_positions = start + seq * SPAN_ROWS + jnp.arange(SPAN_ROWS, dtype=jnp.int32)
    cand_positions = start + SPAN_ROWS * 4 * NY + jnp.arange(CAND_ROWS, dtype=jnp.int32)
    positions = jnp.concatenate([span_positions, cand_positions]).astype(jnp.float32)
    frequency = rope_base ** (-(jnp.arange(half, dtype=jnp.float32) * 2.0 / HD))
    angles = frequency[:, None] * positions[None, :]
    cosine, sine = jnp.cos(angles), jnp.sin(angles)
    q_cosine = jnp.concatenate([cosine, cosine], axis=0).T
    q_sine = jnp.concatenate([-sine, sine], axis=0).T

    place = jnp.stack([at_x, at_z])
    wkv_t = jnp.concatenate([wk.T, wv.T], axis=0)
    q, kv_half = project(
        layout, place, blocks, norm_gain[:, None], wq, wkv_t, q_gain[None, :], q_cosine, q_sine
    )

    def sources(core):
        return jnp.stack(
            [
                ((at_y + NY - ky) % NY * 2 + (at_near + near) % 2) * 2 + core
                for ky in range(NY)
                for near in range(2)
            ]
        )

    from_near, from_far = sources(at_core), sources(1 - at_core)
    limits = start - jnp.arange(4 * NY, dtype=jnp.int32) * cache_rows
    wo_block, q, kv_half = after((wo_block, q, kv_half))
    wo_all = lax.all_gather(wo_block, "seq")

    other_half = swap_pair(kv_half)
    state = attend_cache(limits, q, cache_all, 0, None)
    kv_new = join_pair(kv_half, other_half, parity)
    raw = kv_new[:HD].astype(jnp.float32)
    raw = raw * lax.rsqrt(jnp.mean(raw * raw, axis=0, keepdims=True) + epsilon) * k_gain[:, None]
    front, back = raw[:half], raw[half:]
    new_keys = jnp.concatenate(
        [front * cosine - back * sine, back * cosine + front * sine], axis=0
    ).astype(jnp.bfloat16)
    new_block = jnp.concatenate([new_keys, kv_new[HD:]], axis=0)
    new_block, state = after((new_block, state))
    span_block, own_block = new_block[:, :SPAN_ROWS], new_block[:, SPAN_ROWS:]
    other_near = swap_near(span_block)
    state = attend_cache(limits, q, cache_all, 1, state)
    other_near, state = after((other_near, state))
    span_parts = spread_y(jnp.stack([span_block, other_near]))
    state = attend_cache(limits, q, cache_all, 2, state)
    state = attend_cache(limits, q, cache_all, 3, state)
    span_parts, state = after((span_parts, state))
    span_near = jnp.stack(span_parts)
    span_far = swap_core(span_near)
    span_shape = (2 * NY, 2 * HD, SPAN_ROWS)
    span_near, span_far = span_near.reshape(span_shape), span_far.reshape(span_shape)
    state = attend_span((seq - from_near) * SPAN_ROWS, q, span_near, None, state)
    attended = attend_span((seq - from_far) * SPAN_ROWS, q, span_far, own_block, state)

    a2, a1, a3 = move_x(attended, 2), move_x(attended, 1), move_x(attended, 3)
    picks = jnp.stack([(at_z + kz) % NZ * 4 for kz in range(NZ)])
    pieces = project_out(picks, [attended, a1, a2, a3], wo_all)
    result = pieces[0]
    for kz in (2, 1, 3):
        result = result + move_z(pieces[kz], kz).astype(jnp.float32)
    span_out = result[:, :SPAN_ROWS].astype(jnp.bfloat16).T
    valid = jnp.arange(CAND_ROWS, dtype=jnp.int32)[None, :] < cand_len[0]
    cand_out = jnp.where(valid, result[:, SPAN_ROWS:], 0.0).astype(jnp.bfloat16).T[None]
    return span_out, cand_out


def solution(mesh):
    in_specs = (
        P("seq", "head"),
        P("seq", None, "head"),
        P("seq"),
        P(),
        P(),
        P(None, "head"),
        P(None, "head"),
        P(None, "head"),
        P(),
        P(),
        P("head", None),
        P("seq", "head"),
        P("seq", "head"),
    )
    out_specs = (P("seq", "head"), P("seq", None, "head"))
    return jax.shard_map(
        per_device, mesh=mesh, in_specs=in_specs, out_specs=out_specs, check_vma=False
    )
```

```python
import functools
import math

import jax
import jax.numpy as jnp
from jax import lax
from jax.experimental import pallas as pl
from jax.experimental.pallas import tpu as pltpu
from jax.sharding import PartitionSpec as P

epsilon = 1e-06
rope_base = 1000000.0
NX = 4
NZ = 4
HEADS = 4
HD = 128
SPAN_ROWS = 256
CAND_ROWS = 128
ROWS = SPAN_ROWS + CAND_ROWS
LOG2E = 1.4426950408889634
NY = 4
MIB = 1024 * 1024


def move_x(block, step):
    route = []
    for x in range(NX):
        for z in range(NZ):
            route.append((x * NZ + z, (x + step) % NX * NZ + z))
    return lax.ppermute(block, "head", route)


def move_z(block, step):
    route = []
    for x in range(NX):
        for z in range(NZ):
            route.append((x * NZ + z, x * NZ + (z + step) % NZ))
    return lax.ppermute(block, "head", route)


def swap_pair(block):
    return lax.ppermute(block, "head", [(h, h ^ 1) for h in range(NX * NZ)])


def move_y(block, step):
    return lax.ppermute(block, "seq", [(s, (s + 4 * step) % (4 * NY)) for s in range(4 * NY)])


def swap_near(block):
    return lax.ppermute(block, "seq", [(s, s ^ 2) for s in range(4 * NY)])


def swap_core(block):
    return lax.ppermute(block, "seq", [(s, s ^ 1) for s in range(4 * NY)])


def spread_y(near):
    others = [move_y(near, step) for step in (2, 1, 3)]
    return [near, others[1], others[0], others[2]]


def after(values, *earlier):
    return lax.optimization_barrier((values, earlier))[0]


def whole_spec():
    return pl.BlockSpec(memory_space=pltpu.VMEM)


def project_kernel(layout, place, *refs):
    count = len({ref for ref, _ in layout.values()})
    blocks = refs[:count]
    gain, wq, wkv_t, q_gain, cosine, sine, q_out, kv_out, normed = refs[count:]
    features = gain.shape[0]
    width = features // (NX * NZ)
    total = jnp.zeros((1, ROWS), jnp.float32)
    for block in blocks:
        values = block[:, :ROWS].astype(jnp.float32)
        total = total + jnp.sum(values * values, axis=0, keepdims=True)
    scale = lax.rsqrt(total / features + epsilon)
    for (kx, kz), (ref, part) in layout.items():
        x = lax.rem(place[0] + NX - kx, NX)
        z = lax.rem(place[1] + NZ - kz, NZ)
        rows = pl.ds(pl.multiple_of((x * NZ + z) * width, width), width)
        values = blocks[ref][part * width : (part + 1) * width, :ROWS].astype(jnp.float32)
        normed[rows, :] = (values * scale * gain[rows, :]).astype(jnp.bfloat16)
    kv_out[...] = jnp.dot(
        wkv_t[...], normed[...], preferred_element_type=jnp.float32
    ).astype(jnp.bfloat16)
    queries = lax.dot_general(
        normed[...], wq[...], (((0,), (0,)), ((), ())), preferred_element_type=jnp.float32
    )
    for head in range(HEADS):
        values = queries[:, head * HD : (head + 1) * HD]
        mean_square = jnp.mean(values * values, axis=1, keepdims=True)
        values = values * lax.rsqrt(mean_square + epsilon) * q_gain[...]
        turned = values * cosine[...] + pltpu.roll(values, HD // 2, 1) * sine[...]
        q_out[head] = turned.astype(jnp.bfloat16)


def project(layout, place, blocks, gain, wq, wkv_t, q_gain, cosine, sine):
    vmem = whole_spec()
    return pl.pallas_call(
        functools.partial(project_kernel, layout),
        in_specs=[pl.BlockSpec(memory_space=pltpu.SMEM)] + [vmem] * (len(blocks) + 6),
        out_specs=[vmem, vmem],
        out_shape=[
            jax.ShapeDtypeStruct((HEADS, ROWS, HD), jnp.bfloat16),
            jax.ShapeDtypeStruct((wkv_t.shape[0], ROWS), jnp.bfloat16),
        ],
        scratch_shapes=[pltpu.VMEM((wq.shape[0], ROWS), jnp.bfloat16)],
        compiler_params=pltpu.CompilerParams(vmem_limit_bytes=30 * MIB),
        cost_estimate=pl.CostEstimate(
            flops=2 * ROWS * 5120 * 640, bytes_accessed=12_000_000, transcendentals=0
        ),
    )(place, *blocks, gain, wq, wkv_t, q_gain, cosine, sine)


def fold_all(units, keys, values, top, total, keep):
    scale = LOG2E / math.sqrt(HD)
    ready = jnp.dot(units[0][2], keys, preferred_element_type=jnp.float32)
    for index, (head, rows, _) in enumerate(units):
        scores = ready * scale
        if index + 1 < len(units):
            ready = jnp.dot(units[index + 1][2], keys, preferred_element_type=jnp.float32)
        if keep is not None:
            scores = jnp.where(keep, scores, -1e30)
        old_top = top[head, rows]
        new_top = jnp.maximum(old_top, jnp.max(scores, axis=1, keepdims=True))
        factor = jnp.exp2(old_top - new_top)
        weights = jnp.exp2(scores - new_top[:, :1]).astype(jnp.bfloat16)
        added = lax.dot_general(
            weights, values, (((1,), (1,)), ((), ())), preferred_element_type=jnp.float32
        )
        total[head, rows] = total[head, rows] * jnp.concatenate([factor, factor], axis=1) + added
        top[head, rows] = new_top


def whole_units(q):
    return [(head, slice(0, ROWS), q[head]) for head in range(HEADS)]


def side_by_side(kv, low, high):
    return jnp.concatenate([kv[i, low:high, :] for i in range(kv.shape[0])], axis=1)


def cache_kernel(first, limits, q, kv, *refs):
    top, total = refs[-2:]
    if first is None:
        top[...] = jnp.full(top.shape, -1e30, jnp.float32)
        total[...] = jnp.zeros(total.shape, jnp.float32)
        first = 0
    else:
        top[...] = refs[0][...]
        total[...] = refs[1][...]
    count, _, width = kv.shape
    slot = lax.broadcasted_iota(jnp.int32, (HD, width), 1)
    counted = jnp.concatenate(
        [(slot < limits[first + i]).astype(jnp.bfloat16) for i in range(count)], axis=1
    )
    values = jnp.concatenate([side_by_side(kv, HD, 2 * HD), counted], axis=0)
    fold_all(whole_units(q), side_by_side(kv, 0, HD), values, top, total, None)


STATE = [
    jax.ShapeDtypeStruct((HEADS, ROWS, HD), jnp.float32),
    jax.ShapeDtypeStruct((HEADS, ROWS, 2 * HD), jnp.float32),
]


def whole_block(shape):
    return pl.BlockSpec(shape, lambda i: (0,) * len(shape))


def attend_cache(limits, q, kv, part, state):
    count = kv.shape[0] // 2
    state_specs = [whole_block(s.shape) for s in STATE]
    return pl.pallas_call(
        functools.partial(cache_kernel, None if state is None else part * count),
        grid=(1,),
        in_specs=[
            pl.BlockSpec(memory_space=pltpu.SMEM),
            whole_block(q.shape),
            pl.BlockSpec((count,) + kv.shape[1:], lambda i: (part, 0, 0)),
        ] + ([] if state is None else state_specs),
        out_specs=state_specs,
        out_shape=STATE,
        compiler_params=pltpu.CompilerParams(vmem_limit_bytes=28 * MIB),
        cost_estimate=pl.CostEstimate(
            flops=4 * HEADS * ROWS * HD * 2048, bytes_accessed=5_000_000, transcendentals=HEADS * ROWS * 2048
        ),
    )(limits, q, kv, *([] if state is None else state))


def span_kernel(rows, ahead, q, kv, *refs):
    last = rows is not None
    extra = 1 if last and rows.start else 0
    top, total = refs[-2:]
    top[...] = refs[extra][...]
    total[...] = refs[extra + 1][...]
    rows = rows if last else slice(0, ROWS)
    count, _, width = kv.shape
    keep = None
    if rows.start == 0:
        row = lax.broadcasted_iota(jnp.int32, (rows.stop, width), 0)
        slot = lax.broadcasted_iota(jnp.int32, (rows.stop, width), 1)
        beyond = jnp.where(row >= SPAN_ROWS, -(1 << 24), slot - row)
        keep = jnp.concatenate([beyond <= ahead[i] for i in range(count)], axis=1)
    units = [(head, rows, q[head, rows]) for head in range(HEADS)]
    values = side_by_side(kv, HD, 2 * HD)
    values = jnp.concatenate([values, jnp.ones_like(values)], axis=0)
    fold_all(units, side_by_side(kv, 0, HD), values, top, total, keep)
    if extra:
        own = refs[0]
        row = lax.broadcasted_iota(jnp.int32, (CAND_ROWS, CAND_ROWS), 0)
        slot = lax.broadcasted_iota(jnp.int32, (CAND_ROWS, CAND_ROWS), 1)
        values = own[HD:, :]
        values = jnp.concatenate([values, jnp.ones_like(values)], axis=0)
        fold_all(units, own[:HD, :], values, top, total, slot <= row)
    if last:
        out = refs[extra + 2]
        for head in range(HEADS):
            attended = total[head, rows, :HD] / total[head, rows, HD:]
            out[head * HD : (head + 1) * HD, :] = attended.T.astype(jnp.bfloat16)


def attend_span(ahead, q, kv, own, state, rows):
    state_specs = [whole_block(s.shape) for s in STATE]
    count = ROWS
    if rows is not None:
        count = rows.stop - rows.start
        out_specs = whole_block((HEADS * HD, count))
        out_shape = jax.ShapeDtypeStruct((HEADS * HD, count), jnp.bfloat16)
    else:
        out_specs, out_shape = state_specs, STATE
    return pl.pallas_call(
        functools.partial(span_kernel, rows),
        grid=(1,),
        in_specs=[
            pl.BlockSpec(memory_space=pltpu.SMEM),
            whole_block(q.shape),
            whole_block(kv.shape),
        ] + ([] if own is None else [whole_block(own.shape)]) + state_specs,
        out_specs=out_specs,
        out_shape=out_shape,
        scratch_shapes=[] if rows is None else [pltpu.VMEM(s.shape, s.dtype) for s in STATE],
        compiler_params=pltpu.CompilerParams(vmem_limit_bytes=32 * MIB),
        cost_estimate=pl.CostEstimate(
            flops=4 * HEADS * count * HD * 2048, bytes_accessed=5_000_000, transcendentals=HEADS * count * 2048
        ),
    )(ahead, q, kv, *([] if own is None else [own]), *state)


def output_kernel(picks, *refs):
    attended, (near, far), outs = refs[:NX], refs[NX : NX + 2], refs[NX + 2 :]
    for kz in range(NZ):
        ky = picks[kz]
        total = None
        for kx in range(NX):
            rows = jnp.concatenate(
                [half[ky, i, kx] for half in (near, far) for i in range(2)], axis=0
            )
            term = jnp.dot(rows, attended[kx][...], preferred_element_type=jnp.float32)
            total = term if total is None else total + term
        outs[kz][...] = total.astype(outs[kz].dtype)


def project_out(picks, attended, near, far):
    width = 4 * near.shape[3]
    return pl.pallas_call(
        output_kernel,
        in_specs=[pl.BlockSpec(memory_space=pltpu.SMEM)] + [whole_spec()] * (NX + 2),
        out_specs=[whole_spec()] * NZ,
        out_shape=[
            jax.ShapeDtypeStruct((width, attended[0].shape[1]), jnp.bfloat16 if kz else jnp.float32)
            for kz in range(NZ)
        ],
        compiler_params=pltpu.CompilerParams(vmem_limit_bytes=20 * MIB),
        cost_estimate=pl.CostEstimate(
            flops=2 * ROWS * 2048 * 1280, bytes_accessed=8_000_000, transcendentals=0
        ),
    )(picks, *attended, near, far)


def join_pair(mine, other, parity):
    half = mine.shape[0] // 2
    low = jnp.where(parity == 0, mine, other)
    high = jnp.where(parity == 0, other, mine)
    return jnp.concatenate([low[:half], high[:half], low[half:], high[half:]], axis=0)


def per_device(
    span_x, cand_x, cand_len, offset, norm_gain, wq, wk, wv, q_gain, k_gain, wo, cache_k, cache_v
):
    head = lax.axis_index("head").astype(jnp.int32)
    seq = lax.axis_index("seq").astype(jnp.int32)
    at_x, at_z = head // NZ, head % NZ
    at_y, at_near, at_core = seq // 4, seq // 2 % 2, seq % 2
    parity = head % 2
    width = span_x.shape[1]
    half = HD // 2
    start = offset[0]

    part = width // 4
    own_x = jnp.concatenate([span_x.T, cand_x[0].T], axis=1)
    z1, z3 = move_z(own_x, 1), move_z(own_x, 3)
    x1, x3 = move_x(own_x, 1), move_x(own_x, 3)
    cache_rows = cache_k.shape[0]
    seen = (seq * cache_rows + jnp.arange(cache_rows, dtype=jnp.int32) < start)[None, :]
    keys_t, values_t = cache_k.T, cache_v.T
    cache_half = jnp.concatenate(
        [jnp.where(seen, keys_t, keys_t[:, :1]), jnp.where(seen, values_t, 0)], axis=0
    )
    other_cache = swap_pair(cache_half)

    z1, z3, x1, x3, other_cache, own_x = after((z1, z3, x1, x3, other_cache, own_x))
    cache_block = join_pair(cache_half, other_cache, parity)
    other_near = swap_near(cache_block)
    z2 = move_z(own_x, 2)
    pair = jnp.concatenate([z1, z3], axis=0)
    x1_pair, x3_pair = move_x(pair, 1), move_x(pair, 3)
    shares = []
    for kx in range(NX):
        column = ((at_x + kx) % NX * NZ * 4 + seq) * part
        share = lax.dynamic_slice(wo, (0, column), (wo.shape[0], part)).T
        shares.append(share.reshape(part, 4, HD).transpose(1, 0, 2).reshape(width, HD))
    x2 = move_x(jnp.concatenate([own_x, shares[2]], axis=1), 2)

    z2, x1_pair, x3_pair, x2, other_near, shares = after(
        (z2, x1_pair, x3_pair, x2, other_near, shares)
    )
    x1_z2 = move_x(jnp.concatenate([z2, shares[1]], axis=1), 1)
    x3_z2 = move_x(jnp.concatenate([z2, shares[3]], axis=1), 3)
    x2_z = move_x(jnp.concatenate([pair, z2], axis=0), 2)
    cache_near = jnp.stack([cache_block, other_near])
    cache_parts = [cache_near, move_y(cache_near, 1), None, move_y(cache_near, 3)]
    cache_parts[2] = move_y(cache_near, 2)
    x1_z2, x3_z2, x2_z, cache_parts[1], cache_parts[3] = after(
        (x1_z2, x3_z2, x2_z, cache_parts[1], cache_parts[3])
    )
    wo_block = jnp.stack(
        [shares[0].reshape(4, part, HD).transpose(1, 0, 2).reshape(part, 4 * HD)]
        + [
            b[:, ROWS:].reshape(4, part, HD).transpose(1, 0, 2).reshape(part, 4 * HD)
            for b in (x1_z2, x2, x3_z2)
        ]
    )
    wo_near = jnp.stack([wo_block, swap_near(wo_block)])
    blocks = [own_x, z1, z3, z2, x1, x2, x3, x1_pair, x3_pair, x1_z2, x3_z2, x2_z]
    layout = {(0, 0): (0, 0), (0, 1): (1, 0), (0, 3): (2, 0), (0, 2): (3, 0)}
    layout.update({(1, 0): (4, 0), (2, 0): (5, 0), (3, 0): (6, 0)})
    layout.update({(1, 1): (7, 0), (1, 3): (7, 1), (3, 1): (8, 0), (3, 3): (8, 1)})
    layout.update({(1, 2): (9, 0), (3, 2): (10, 0)})
    layout.update({(2, 1): (11, 0), (2, 3): (11, 1), (2, 2): (11, 2)})

    span_positions = start + seq * SPAN_ROWS + jnp.arange(SPAN_ROWS, dtype=jnp.int32)
    cand_positions = start + SPAN_ROWS * 4 * NY + jnp.arange(CAND_ROWS, dtype=jnp.int32)
    positions = jnp.concatenate([span_positions, cand_positions]).astype(jnp.float32)
    frequency = rope_base ** (-(jnp.arange(half, dtype=jnp.float32) * 2.0 / HD))
    angles = frequency[:, None] * positions[None, :]
    cosine, sine = jnp.cos(angles), jnp.sin(angles)
    q_cosine = jnp.concatenate([cosine, cosine], axis=0).T
    q_sine = jnp.concatenate([-sine, sine], axis=0).T

    place = jnp.stack([at_x, at_z])
    wkv_t = jnp.concatenate([wk.T, wv.T], axis=0)
    q, kv_half = project(
        layout, place, blocks, norm_gain[:, None], wq, wkv_t, q_gain[None, :], q_cosine, q_sine
    )

    def sources(core):
        return jnp.stack(
            [
                ((at_y + NY - ky) % NY * 2 + (at_near + near) % 2) * 2 + core
                for ky in range(NY)
                for near in range(2)
            ]
        )

    from_near, from_far = sources(at_core), sources(1 - at_core)
    near_limits = start - from_near * cache_rows
    far_limits = start - from_far * cache_rows
    cache_parts, wo_near = after((cache_parts, wo_near))
    wo_parts = [wo_near, move_y(wo_near, 1), None, move_y(wo_near, 3)]
    cache_near = jnp.stack(cache_parts)
    cache_far = swap_core(cache_near)
    cache_shape = (2 * NY, 2 * HD, cache_rows)
    cache_near, cache_far = cache_near.reshape(cache_shape), cache_far.reshape(cache_shape)

    other_half = swap_pair(kv_half)
    state = attend_cache(near_limits, q, cache_near, 0, None)
    kv_new = join_pair(kv_half, other_half, parity)
    raw = kv_new[:HD].astype(jnp.float32)
    raw = raw * lax.rsqrt(jnp.mean(raw * raw, axis=0, keepdims=True) + epsilon) * k_gain[:, None]
    front, back = raw[:half], raw[half:]
    new_keys = jnp.concatenate(
        [front * cosine - back * sine, back * cosine + front * sine], axis=0
    ).astype(jnp.bfloat16)
    new_block = jnp.concatenate([new_keys, kv_new[HD:]], axis=0)
    new_block, state = after((new_block, state))
    span_block, own_block = new_block[:, :SPAN_ROWS], new_block[:, SPAN_ROWS:]
    other_near = swap_near(span_block)
    state = attend_cache(near_limits, q, cache_near, 1, state)
    other_near, state, wo_near, wo_parts[1], wo_parts[3] = after(
        (other_near, state, wo_near, wo_parts[1], wo_parts[3])
    )
    span_parts = spread_y(jnp.stack([span_block, other_near]))
    state = attend_cache(far_limits, q, cache_far, 0, state)
    state = attend_cache(far_limits, q, cache_far, 1, state)
    span_parts, state, wo_near = after((span_parts, state, wo_near))
    wo_parts[2] = move_y(wo_near, 2)
    span_near = jnp.stack(span_parts)
    span_far = swap_core(span_near)
    span_shape = (2 * NY, 2 * HD, SPAN_ROWS)
    span_near, span_far = span_near.reshape(span_shape), span_far.reshape(span_shape)
    state = attend_span((seq - from_near) * SPAN_ROWS, q, span_near, None, state, None)
    ahead = (seq - from_far) * SPAN_ROWS
    picks = jnp.stack([(at_y - at_z - kz + 2 * NZ) % NY for kz in range(NZ)])

    def over_x(attended):
        a2, a1, a3 = move_x(attended, 2), move_x(attended, 1), move_x(attended, 3)
        return [attended, a1, a2, a3]

    def over_z(pieces):
        z2, z1, z3 = move_z(pieces[2], 2), move_z(pieces[1], 1), move_z(pieces[3], 3)
        return [pieces[0], z1, z2, z3]

    def in_order(pieces):
        result = sum(piece.astype(jnp.float32) for piece in pieces)
        result = result.reshape(2, 2, part, result.shape[1])
        result = jnp.where(at_core == 1, result[::-1], result)
        result = jnp.where(at_near == 1, result[:, ::-1], result)
        return result.transpose(1, 0, 2, 3).reshape(width, result.shape[3])

    cand = attend_span(ahead, q, span_far, own_block, state, slice(SPAN_ROWS, ROWS))
    state, wo_parts = after(state, cand), after(wo_parts, cand)
    cand = over_x(cand)
    wo_near = jnp.stack(wo_parts)
    wo_far = swap_core(wo_near)
    span = over_x(attend_span(ahead, q, span_far, None, state, slice(0, SPAN_ROWS)))
    cand = over_z(project_out(picks, cand, wo_near, wo_far))
    span, cand = after((span, cand))
    span = over_z(project_out(picks, span, wo_near, wo_far))
    span_out = in_order(span).astype(jnp.bfloat16).T
    valid = jnp.arange(CAND_ROWS, dtype=jnp.int32)[None, :] < cand_len[0]
    cand_out = jnp.where(valid, in_order(cand), 0.0).astype(jnp.bfloat16).T[None]
    return span_out, cand_out


def solution(mesh):
    in_specs = (
        P("seq", "head"),
        P("seq", None, "head"),
        P("seq"),
        P(),
        P(),
        P(None, "head"),
        P(None, "head"),
        P(None, "head"),
        P(),
        P(),
        P("head", None),
        P("seq", "head"),
        P("seq", "head"),
    )
    out_specs = (P("seq", "head"), P("seq", None, "head"))
    return jax.shard_map(
        per_device, mesh=mesh, in_specs=in_specs, out_specs=out_specs, check_vma=False
    )
```

```python
import functools
import math

import jax
import jax.numpy as jnp
from jax import lax
from jax.experimental import pallas as pl
from jax.experimental.pallas import tpu as pltpu
from jax.sharding import PartitionSpec as P

epsilon = 1e-06
rope_base = 1000000.0
NX = 4
NZ = 4
HEADS = 4
HD = 128
SPAN_ROWS = 256
CAND_ROWS = 128
ROWS = SPAN_ROWS + CAND_ROWS
LOG2E = 1.4426950408889634
NY = 4
MIB = 1024 * 1024


def move_x(block, step):
    route = []
    for x in range(NX):
        for z in range(NZ):
            route.append((x * NZ + z, (x + step) % NX * NZ + z))
    return lax.ppermute(block, "head", route)


def move_z(block, step):
    route = []
    for x in range(NX):
        for z in range(NZ):
            route.append((x * NZ + z, x * NZ + (z + step) % NZ))
    return lax.ppermute(block, "head", route)


def swap_pair(block):
    return lax.ppermute(block, "head", [(h, h ^ 1) for h in range(NX * NZ)])


def move_y(block, step):
    return lax.ppermute(block, "seq", [(s, (s + 4 * step) % (4 * NY)) for s in range(4 * NY)])


def swap_near(block):
    return lax.ppermute(block, "seq", [(s, s ^ 2) for s in range(4 * NY)])


def swap_core(block):
    return lax.ppermute(block, "seq", [(s, s ^ 1) for s in range(4 * NY)])


def spread_y(near):
    others = [move_y(near, step) for step in (2, 1, 3)]
    return [near, others[1], others[0], others[2]]


def after(values, *earlier):
    return lax.optimization_barrier((values, earlier))[0]


def whole_spec():
    return pl.BlockSpec(memory_space=pltpu.VMEM)


def project_kernel(layout, place, *refs):
    count = len({ref for ref, _ in layout.values()})
    blocks = refs[:count]
    gain, wq, wkv_t, q_gain, cosine, sine, q_out, kv_out, normed = refs[count:]
    features = gain.shape[0]
    width = features // (NX * NZ)
    total = jnp.zeros((1, ROWS), jnp.float32)
    for block in blocks:
        values = block[:, :ROWS].astype(jnp.float32)
        total = total + jnp.sum(values * values, axis=0, keepdims=True)
    scale = lax.rsqrt(total / features + epsilon)
    for (kx, kz), (ref, part) in layout.items():
        x = lax.rem(place[0] + NX - kx, NX)
        z = lax.rem(place[1] + NZ - kz, NZ)
        rows = pl.ds(pl.multiple_of((x * NZ + z) * width, width), width)
        values = blocks[ref][part * width : (part + 1) * width, :ROWS].astype(jnp.float32)
        normed[rows, :] = (values * scale * gain[rows, :]).astype(jnp.bfloat16)
    kv_out[...] = jnp.dot(
        wkv_t[...], normed[...], preferred_element_type=jnp.float32
    ).astype(jnp.bfloat16)
    queries = lax.dot_general(
        normed[...], wq[...], (((0,), (0,)), ((), ())), preferred_element_type=jnp.float32
    )
    for head in range(HEADS):
        values = queries[:, head * HD : (head + 1) * HD]
        mean_square = jnp.mean(values * values, axis=1, keepdims=True)
        values = values * lax.rsqrt(mean_square + epsilon) * q_gain[...]
        turned = values * cosine[...] + pltpu.roll(values, HD // 2, 1) * sine[...]
        q_out[head] = turned.astype(jnp.bfloat16)


def project(layout, place, blocks, gain, wq, wkv_t, q_gain, cosine, sine):
    vmem = whole_spec()
    return pl.pallas_call(
        functools.partial(project_kernel, layout),
        in_specs=[pl.BlockSpec(memory_space=pltpu.SMEM)] + [vmem] * (len(blocks) + 6),
        out_specs=[vmem, vmem],
        out_shape=[
            jax.ShapeDtypeStruct((HEADS, ROWS, HD), jnp.bfloat16),
            jax.ShapeDtypeStruct((wkv_t.shape[0], ROWS), jnp.bfloat16),
        ],
        scratch_shapes=[pltpu.VMEM((wq.shape[0], ROWS), jnp.bfloat16)],
        compiler_params=pltpu.CompilerParams(vmem_limit_bytes=20 * MIB),
        cost_estimate=pl.CostEstimate(
            flops=2 * ROWS * 5120 * 640, bytes_accessed=12_000_000, transcendentals=0
        ),
    )(place, *blocks, gain, wq, wkv_t, q_gain, cosine, sine)


def fold_all(units, keys, values, top, total, keep):
    scale = LOG2E / math.sqrt(HD)
    ready = jnp.dot(units[0][2], keys, preferred_element_type=jnp.float32)
    for index, (head, rows, _) in enumerate(units):
        scores = ready * scale
        if index + 1 < len(units):
            ready = jnp.dot(units[index + 1][2], keys, preferred_element_type=jnp.float32)
        if keep is not None:
            scores = jnp.where(keep, scores, -1e30)
        old_top = top[head, rows]
        new_top = jnp.maximum(old_top, jnp.max(scores, axis=1, keepdims=True))
        factor = jnp.exp2(old_top - new_top)
        weights = jnp.exp2(scores - new_top[:, :1]).astype(jnp.bfloat16)
        added = lax.dot_general(
            weights, values, (((1,), (1,)), ((), ())), preferred_element_type=jnp.float32
        )
        total[head, rows] = total[head, rows] * jnp.concatenate([factor, factor], axis=1) + added
        top[head, rows] = new_top


def whole_units(q):
    return [(head, slice(0, ROWS), q[head]) for head in range(HEADS)]


def side_by_side(kv, low, high):
    return jnp.concatenate([kv[i, low:high, :] for i in range(kv.shape[0])], axis=1)


def cache_kernel(first, limits, q, kv, *refs):
    top, total = refs[-2:]
    if first is None:
        top[...] = jnp.full(top.shape, -1e30, jnp.float32)
        total[...] = jnp.zeros(total.shape, jnp.float32)
        first = 0
    else:
        top[...] = refs[0][...]
        total[...] = refs[1][...]
    count, _, width = kv.shape
    slot = lax.broadcasted_iota(jnp.int32, (HD, width), 1)
    counted = jnp.concatenate(
        [(slot < limits[first + i]).astype(jnp.bfloat16) for i in range(count)], axis=1
    )
    values = jnp.concatenate([side_by_side(kv, HD, 2 * HD), counted], axis=0)
    fold_all(whole_units(q), side_by_side(kv, 0, HD), values, top, total, None)


STATE = [
    jax.ShapeDtypeStruct((HEADS, ROWS, HD), jnp.float32),
    jax.ShapeDtypeStruct((HEADS, ROWS, 2 * HD), jnp.float32),
]


def whole_block(shape):
    return pl.BlockSpec(shape, lambda i: (0,) * len(shape))


def attend_cache(limits, q, kv, part, state):
    count = kv.shape[0] // 2
    state_specs = [whole_block(s.shape) for s in STATE]
    return pl.pallas_call(
        functools.partial(cache_kernel, None if state is None else part * count),
        grid=(1,),
        in_specs=[
            pl.BlockSpec(memory_space=pltpu.SMEM),
            whole_block(q.shape),
            pl.BlockSpec((count,) + kv.shape[1:], lambda i: (part, 0, 0)),
        ] + ([] if state is None else state_specs),
        out_specs=state_specs,
        out_shape=STATE,
        compiler_params=pltpu.CompilerParams(vmem_limit_bytes=22 * MIB),
        cost_estimate=pl.CostEstimate(
            flops=4 * HEADS * ROWS * HD * 2048, bytes_accessed=5_000_000, transcendentals=HEADS * ROWS * 2048
        ),
    )(limits, q, kv, *([] if state is None else state))


def span_kernel(rows, ahead, q, kv, *refs):
    last = rows is not None
    extra = 1 if last else 0
    top, total = refs[-2:]
    top[...] = refs[extra][...]
    total[...] = refs[extra + 1][...]
    rows = rows if last else slice(0, ROWS)
    count, _, width = kv.shape
    keep = None
    if rows.start == 0:
        row = lax.broadcasted_iota(jnp.int32, (rows.stop, width), 0)
        slot = lax.broadcasted_iota(jnp.int32, (rows.stop, width), 1)
        beyond = jnp.where(row >= SPAN_ROWS, -(1 << 24), slot - row)
        keep = jnp.concatenate([beyond <= ahead[i] for i in range(count)], axis=1)
    units = [(head, rows, q[head, rows]) for head in range(HEADS)]
    values = side_by_side(kv, HD, 2 * HD)
    values = jnp.concatenate([values, jnp.ones_like(values)], axis=0)
    fold_all(units, side_by_side(kv, 0, HD), values, top, total, keep)
    if extra:
        own = refs[0]
        row = lax.broadcasted_iota(jnp.int32, (CAND_ROWS, CAND_ROWS), 0)
        slot = lax.broadcasted_iota(jnp.int32, (CAND_ROWS, CAND_ROWS), 1)
        values = own[HD:, :]
        values = jnp.concatenate([values, jnp.ones_like(values)], axis=0)
        cand = slice(SPAN_ROWS, ROWS)
        units = [(head, cand, q[head, cand]) for head in range(HEADS)]
        fold_all(units, own[:HD, :], values, top, total, slot <= row)
    if last:
        out = refs[extra + 2]
        for head in range(HEADS):
            attended = total[head, rows, :HD] / total[head, rows, HD:]
            out[head * HD : (head + 1) * HD, :] = attended.T.astype(jnp.bfloat16)


def attend_span(ahead, q, kv, own, state, rows):
    state_specs = [whole_block(s.shape) for s in STATE]
    count = ROWS
    if rows is not None:
        count = rows.stop - rows.start
        out_specs = whole_block((HEADS * HD, count))
        out_shape = jax.ShapeDtypeStruct((HEADS * HD, count), jnp.bfloat16)
    else:
        out_specs, out_shape = state_specs, STATE
    return pl.pallas_call(
        functools.partial(span_kernel, rows),
        grid=(1,),
        in_specs=[
            pl.BlockSpec(memory_space=pltpu.SMEM),
            whole_block(q.shape),
            whole_block(kv.shape),
        ] + ([] if own is None else [whole_block(own.shape)]) + state_specs,
        out_specs=out_specs,
        out_shape=out_shape,
        scratch_shapes=[] if rows is None else [pltpu.VMEM(s.shape, s.dtype) for s in STATE],
        compiler_params=pltpu.CompilerParams(vmem_limit_bytes=20 * MIB),
        cost_estimate=pl.CostEstimate(
            flops=4 * HEADS * count * HD * 2048, bytes_accessed=5_000_000, transcendentals=HEADS * count * 2048
        ),
    )(ahead, q, kv, *([] if own is None else [own]), *state)


def terms_of(wo, attended):
    return lax.dot_general(
        wo[...], attended[...], (((0,), (0,)), ((), ())), preferred_element_type=jnp.float32
    )


def far_kernel(ids, attended, wo, low, high):
    terms = terms_of(wo, attended).astype(jnp.bfloat16)
    half = terms.shape[0] // 2
    low[...] = terms[:half]
    high[...] = terms[half:]


def own_kernel(ids, attended, wo, out):
    out[...] = terms_of(wo, attended)


def near_kernel(ids, attended, wo_next, wo_last, low, high, to_next, to_last):
    half = low.shape[0]
    terms = terms_of(wo_next, attended)
    to_next[:half, :] = (terms[:half] + low[...].astype(jnp.float32)).astype(jnp.bfloat16)
    to_next[half:, :] = terms[half:].astype(jnp.bfloat16)
    terms = terms_of(wo_last, attended)
    to_last[:half, :] = terms[:half].astype(jnp.bfloat16)
    to_last[half:, :] = (terms[half:] + high[...].astype(jnp.float32)).astype(jnp.bfloat16)


def output_call(kernel, ids, attended, wo, others, outs):
    groups, width = attended.shape[0], wo.shape[1] // NX
    fixed = lambda shape: pl.BlockSpec(shape, lambda i, ids: (0, 0))
    picked = [
        pl.BlockSpec((groups, width), lambda i, ids, k=k: (0, ids[k])) for k in range(len(ids))
    ]
    return pl.pallas_call(
        kernel,
        grid_spec=pltpu.PrefetchScalarGridSpec(
            num_scalar_prefetch=1,
            grid=(1,),
            in_specs=[fixed(attended.shape)] + picked + [fixed(o.shape) for o in others],
            out_specs=[fixed(o.shape) for o in outs],
        ),
        out_shape=outs,
        compiler_params=pltpu.CompilerParams(vmem_limit_bytes=20 * MIB),
        cost_estimate=pl.CostEstimate(
            flops=2 * len(ids) * groups * width * ROWS, bytes_accessed=3_000_000, transcendentals=0
        ),
    )(jnp.stack(ids), attended, *([wo] * len(ids)), *others)


def far_terms(group, attended, wo):
    half = jax.ShapeDtypeStruct((wo.shape[1] // NX // 2, ROWS), jnp.bfloat16)
    return output_call(far_kernel, [group], attended, wo, [], [half, half])


def own_terms(group, attended, wo):
    out = jax.ShapeDtypeStruct((wo.shape[1] // NX, ROWS), jnp.float32)
    return output_call(own_kernel, [group], attended, wo, [], [out])[0]


def near_terms(next_group, last_group, attended, wo, low, high):
    out = jax.ShapeDtypeStruct((wo.shape[1] // NX, ROWS), jnp.bfloat16)
    return output_call(
        near_kernel, [next_group, last_group], attended, wo, [low, high], [out, out]
    )


def sum_kernel(at_z, mine, first, second, *refs):
    total = refs[NZ]
    total[...] = mine[...] + first[...].astype(jnp.float32) + second[...].astype(jnp.float32)
    width = total.shape[0] // NZ
    for kz in range(NZ):
        row = pl.multiple_of(lax.rem(at_z[0] + kz, NZ) * width, width)
        refs[kz][...] = total[pl.ds(row, width), :].astype(refs[kz].dtype)


def sum_terms(at_z, mine, first, second):
    width = mine.shape[0] // NZ
    return pl.pallas_call(
        sum_kernel,
        grid=(1,),
        in_specs=[pl.BlockSpec(memory_space=pltpu.SMEM)] + [whole_block(mine.shape)] * 3,
        out_specs=[whole_block((width, ROWS))] * NZ,
        out_shape=[
            jax.ShapeDtypeStruct((width, ROWS), jnp.bfloat16 if kz else jnp.float32)
            for kz in range(NZ)
        ],
        scratch_shapes=[pltpu.VMEM(mine.shape, jnp.float32)],
        compiler_params=pltpu.CompilerParams(vmem_limit_bytes=20 * MIB),
        cost_estimate=pl.CostEstimate(flops=2_000_000, bytes_accessed=6_000_000, transcendentals=0),
    )(at_z[None], mine, first, second)


def join_pair(mine, other, parity):
    half = mine.shape[0] // 2
    low = jnp.where(parity == 0, mine, other)
    high = jnp.where(parity == 0, other, mine)
    return jnp.concatenate([low[:half], high[:half], low[half:], high[half:]], axis=0)


def per_device(
    span_x, cand_x, cand_len, offset, norm_gain, wq, wk, wv, q_gain, k_gain, wo, cache_k, cache_v
):
    head = lax.axis_index("head").astype(jnp.int32)
    seq = lax.axis_index("seq").astype(jnp.int32)
    at_x, at_z = head // NZ, head % NZ
    at_y, at_near, at_core = seq // 4, seq // 2 % 2, seq % 2
    parity = head % 2
    width = span_x.shape[1]
    half = HD // 2
    start = offset[0]

    own_x = jnp.concatenate([span_x.T, cand_x[0].T], axis=1)
    z1, z3 = move_z(own_x, 1), move_z(own_x, 3)
    x1, x3 = move_x(own_x, 1), move_x(own_x, 3)
    cache_rows = cache_k.shape[0]
    seen = (seq * cache_rows + jnp.arange(cache_rows, dtype=jnp.int32) < start)[None, :]
    keys_t, values_t = cache_k.T, cache_v.T
    cache_half = jnp.concatenate(
        [jnp.where(seen, keys_t, keys_t[:, :1]), jnp.where(seen, values_t, 0)], axis=0
    )
    other_cache = swap_pair(cache_half)

    z1, z3, x1, x3, other_cache, own_x = after((z1, z3, x1, x3, other_cache, own_x))
    cache_block = join_pair(cache_half, other_cache, parity)
    other_near = swap_near(cache_block)
    z2 = move_z(own_x, 2)
    pair = jnp.concatenate([z1, z3], axis=0)
    x1_pair, x3_pair = move_x(pair, 1), move_x(pair, 3)
    x2 = move_x(own_x, 2)

    z2, x1_pair, x3_pair, x2, other_near = after((z2, x1_pair, x3_pair, x2, other_near))
    x1_z2, x3_z2 = move_x(z2, 1), move_x(z2, 3)
    x2_z = move_x(jnp.concatenate([pair, z2], axis=0), 2)
    cache_near = jnp.stack([cache_block, other_near])
    cache_parts = [cache_near, move_y(cache_near, 1), None, move_y(cache_near, 3)]
    cache_parts[2] = move_y(cache_near, 2)
    x1_z2, x3_z2, x2_z, cache_parts[1], cache_parts[3] = after(
        (x1_z2, x3_z2, x2_z, cache_parts[1], cache_parts[3])
    )
    blocks = [own_x, z1, z3, z2, x1, x2, x3, x1_pair, x3_pair, x1_z2, x3_z2, x2_z]
    layout = {(0, 0): (0, 0), (0, 1): (1, 0), (0, 3): (2, 0), (0, 2): (3, 0)}
    layout.update({(1, 0): (4, 0), (2, 0): (5, 0), (3, 0): (6, 0)})
    layout.update({(1, 1): (7, 0), (1, 3): (7, 1), (3, 1): (8, 0), (3, 3): (8, 1)})
    layout.update({(1, 2): (9, 0), (3, 2): (10, 0)})
    layout.update({(2, 1): (11, 0), (2, 3): (11, 1), (2, 2): (11, 2)})

    span_positions = start + seq * SPAN_ROWS + jnp.arange(SPAN_ROWS, dtype=jnp.int32)
    cand_positions = start + SPAN_ROWS * 4 * NY + jnp.arange(CAND_ROWS, dtype=jnp.int32)
    positions = jnp.concatenate([span_positions, cand_positions]).astype(jnp.float32)
    frequency = rope_base ** (-(jnp.arange(half, dtype=jnp.float32) * 2.0 / HD))
    angles = frequency[:, None] * positions[None, :]
    cosine, sine = jnp.cos(angles), jnp.sin(angles)
    q_cosine = jnp.concatenate([cosine, cosine], axis=0).T
    q_sine = jnp.concatenate([-sine, sine], axis=0).T

    place = jnp.stack([at_x, at_z])
    wkv_t = jnp.concatenate([wk.T, wv.T], axis=0)
    q, kv_half = project(
        layout, place, blocks, norm_gain[:, None], wq, wkv_t, q_gain[None, :], q_cosine, q_sine
    )

    def sources(core):
        return jnp.stack(
            [
                ((at_y + NY - ky) % NY * 2 + (at_near + near) % 2) * 2 + core
                for ky in range(NY)
                for near in range(2)
            ]
        )

    from_near, from_far = sources(at_core), sources(1 - at_core)
    near_limits = start - from_near * cache_rows
    far_limits = start - from_far * cache_rows
    cache_near = jnp.stack(cache_parts)
    cache_far = swap_core(cache_near)
    cache_shape = (2 * NY, 2 * HD, cache_rows)
    cache_near, cache_far = cache_near.reshape(cache_shape), cache_far.reshape(cache_shape)

    other_half = swap_pair(kv_half)
    state = attend_cache(near_limits, q, cache_near, 0, None)
    kv_new = join_pair(kv_half, other_half, parity)
    raw = kv_new[:HD].astype(jnp.float32)
    raw = raw * lax.rsqrt(jnp.mean(raw * raw, axis=0, keepdims=True) + epsilon) * k_gain[:, None]
    front, back = raw[:half], raw[half:]
    new_keys = jnp.concatenate(
        [front * cosine - back * sine, back * cosine + front * sine], axis=0
    ).astype(jnp.bfloat16)
    new_block = jnp.concatenate([new_keys, kv_new[HD:]], axis=0)
    new_block, state = after((new_block, state))
    span_block, own_block = new_block[:, :SPAN_ROWS], new_block[:, SPAN_ROWS:]
    other_near = swap_near(span_block)
    state = attend_cache(near_limits, q, cache_near, 1, state)
    other_near, state = after((other_near, state))
    span_parts = spread_y(jnp.stack([span_block, other_near]))
    state = attend_cache(far_limits, q, cache_far, 0, state)
    state = attend_cache(far_limits, q, cache_far, 1, state)
    span_parts, state = after((span_parts, state))
    span_near = jnp.stack(span_parts)
    span_far = swap_core(span_near)
    span_shape = (2 * NY, 2 * HD, SPAN_ROWS)
    span_near, span_far = span_near.reshape(span_shape), span_far.reshape(span_shape)
    state = attend_span((seq - from_near) * SPAN_ROWS, q, span_near, None, state, None)
    ahead = (seq - from_far) * SPAN_ROWS
    attended = attend_span(ahead, q, span_far, own_block, state, slice(0, ROWS))

    ids = [(at_x + kx) % NX for kx in range(NX)]
    low, high = far_terms(ids[2], attended, wo)
    low, high = move_x(low, 1), move_x(high, 3)
    mine = own_terms(ids[0], attended, wo)
    low, high, mine = after((low, high, mine))
    to_next, to_last = near_terms(ids[1], ids[3], attended, wo, low, high)
    from_last, from_next = move_x(to_next, 1), move_x(to_last, 3)
    pieces = sum_terms(at_z, mine, from_last, from_next)
    result = pieces[0]
    for kz in (2, 1, 3):
        result = result + move_z(pieces[kz], kz).astype(jnp.float32)
    span_out = result[:, :SPAN_ROWS].astype(jnp.bfloat16).T
    valid = jnp.arange(CAND_ROWS, dtype=jnp.int32)[None, :] < cand_len[0]
    cand_out = jnp.where(valid, result[:, SPAN_ROWS:], 0.0).astype(jnp.bfloat16).T[None]
    return span_out, cand_out


def solution(mesh):
    in_specs = (
        P("seq", "head"),
        P("seq", None, "head"),
        P("seq"),
        P(),
        P(),
        P(None, "head"),
        P(None, "head"),
        P(None, "head"),
        P(),
        P(),
        P("head", None),
        P("seq", "head"),
        P("seq", "head"),
    )
    out_specs = (P("seq", "head"), P("seq", None, "head"))
    return jax.shard_map(
        per_device, mesh=mesh, in_specs=in_specs, out_specs=out_specs, check_vma=False
    )
```

```python
import functools
import math

import jax
import jax.numpy as jnp
from jax import lax
from jax.experimental import pallas as pl
from jax.experimental.pallas import tpu as pltpu
from jax.sharding import PartitionSpec as P

epsilon = 1e-06
rope_base = 1000000.0
NX = 4
NZ = 4
HEADS = 4
HD = 128
SPAN_ROWS = 256
CAND_ROWS = 128
ROWS = SPAN_ROWS + CAND_ROWS
LOG2E = 1.4426950408889634
NY = 4
MIB = 1024 * 1024


def move_x(block, step):
    route = []
    for x in range(NX):
        for z in range(NZ):
            route.append((x * NZ + z, (x + step) % NX * NZ + z))
    return lax.ppermute(block, "head", route)


def move_z(block, step):
    route = []
    for x in range(NX):
        for z in range(NZ):
            route.append((x * NZ + z, x * NZ + (z + step) % NZ))
    return lax.ppermute(block, "head", route)


def swap_pair(block):
    return lax.ppermute(block, "head", [(h, h ^ 1) for h in range(NX * NZ)])


def move_y(block, step):
    return lax.ppermute(block, "seq", [(s, (s + 4 * step) % (4 * NY)) for s in range(4 * NY)])


def swap_near(block):
    return lax.ppermute(block, "seq", [(s, s ^ 2) for s in range(4 * NY)])


def swap_core(block):
    return lax.ppermute(block, "seq", [(s, s ^ 1) for s in range(4 * NY)])


def spread_y(near):
    others = [move_y(near, step) for step in (2, 1, 3)]
    return [near, others[1], others[0], others[2]]


def after(values, *earlier):
    return lax.optimization_barrier((values, earlier))[0]


def whole_spec():
    return pl.BlockSpec(memory_space=pltpu.VMEM)


def project_kernel(layout, place, *refs):
    count = len({ref for ref, _ in layout.values()})
    blocks = refs[:count]
    gain, wq, wkv_t, q_gain, cosine, sine, q_out, kv_out, normed = refs[count:]
    features = gain.shape[0]
    width = features // (NX * NZ)
    total = jnp.zeros((1, ROWS), jnp.float32)
    for block in blocks:
        values = block[:, :ROWS].astype(jnp.float32)
        total = total + jnp.sum(values * values, axis=0, keepdims=True)
    scale = lax.rsqrt(total / features + epsilon)
    for (kx, kz), (ref, part) in layout.items():
        x = lax.rem(place[0] + NX - kx, NX)
        z = lax.rem(place[1] + NZ - kz, NZ)
        rows = pl.ds(pl.multiple_of((x * NZ + z) * width, width), width)
        values = blocks[ref][part * width : (part + 1) * width, :ROWS].astype(jnp.float32)
        normed[rows, :] = (values * scale * gain[rows, :]).astype(jnp.bfloat16)
    kv_out[...] = jnp.dot(
        wkv_t[...], normed[...], preferred_element_type=jnp.float32
    ).astype(jnp.bfloat16)
    queries = lax.dot_general(
        normed[...], wq[...], (((0,), (0,)), ((), ())), preferred_element_type=jnp.float32
    )
    for head in range(HEADS):
        values = queries[:, head * HD : (head + 1) * HD]
        mean_square = jnp.mean(values * values, axis=1, keepdims=True)
        values = values * lax.rsqrt(mean_square + epsilon) * q_gain[...]
        turned = values * cosine[...] + pltpu.roll(values, HD // 2, 1) * sine[...]
        q_out[head] = turned.astype(jnp.bfloat16)


def project(layout, place, blocks, gain, wq, wkv_t, q_gain, cosine, sine):
    vmem = whole_spec()
    return pl.pallas_call(
        functools.partial(project_kernel, layout),
        in_specs=[pl.BlockSpec(memory_space=pltpu.SMEM)] + [vmem] * (len(blocks) + 6),
        out_specs=[vmem, vmem],
        out_shape=[
            jax.ShapeDtypeStruct((HEADS, ROWS, HD), jnp.bfloat16),
            jax.ShapeDtypeStruct((wkv_t.shape[0], ROWS), jnp.bfloat16),
        ],
        scratch_shapes=[pltpu.VMEM((wq.shape[0], ROWS), jnp.bfloat16)],
        compiler_params=pltpu.CompilerParams(vmem_limit_bytes=56 * MIB),
        cost_estimate=pl.CostEstimate(
            flops=2 * ROWS * 5120 * 640, bytes_accessed=12_000_000, transcendentals=0
        ),
    )(place, *blocks, gain, wq, wkv_t, q_gain, cosine, sine)


def fold_all(units, keys, values, top, total, keep):
    scale = LOG2E / math.sqrt(HD)
    ready = jnp.dot(units[0][2], keys, preferred_element_type=jnp.float32)
    for index, (head, rows, _) in enumerate(units):
        scores = ready * scale
        if index + 1 < len(units):
            ready = jnp.dot(units[index + 1][2], keys, preferred_element_type=jnp.float32)
        if keep is not None:
            scores = jnp.where(keep, scores, -1e30)
        old_top = top[head, rows]
        new_top = jnp.maximum(old_top, jnp.max(scores, axis=1, keepdims=True))
        factor = jnp.exp2(old_top - new_top)
        weights = jnp.exp2(scores - new_top[:, :1]).astype(jnp.bfloat16)
        added = lax.dot_general(
            weights, values, (((1,), (1,)), ((), ())), preferred_element_type=jnp.float32
        )
        total[head, rows] = total[head, rows] * jnp.concatenate([factor, factor], axis=1) + added
        top[head, rows] = new_top


def whole_units(q):
    return [(head, slice(0, ROWS), q[head]) for head in range(HEADS)]


def side_by_side(kv, low, high):
    return jnp.concatenate([kv[i, low:high, :] for i in range(kv.shape[0])], axis=1)


def cache_kernel(first, limits, q, kv, *refs):
    top, total = refs[-2:]
    if first is None:
        top[...] = jnp.full(top.shape, -1e30, jnp.float32)
        total[...] = jnp.zeros(total.shape, jnp.float32)
        first = 0
    else:
        top[...] = refs[0][...]
        total[...] = refs[1][...]
    count, _, width = kv.shape
    slot = lax.broadcasted_iota(jnp.int32, (HD, width), 1)
    counted = jnp.concatenate(
        [(slot < limits[first + i]).astype(jnp.bfloat16) for i in range(count)], axis=1
    )
    values = jnp.concatenate([side_by_side(kv, HD, 2 * HD), counted], axis=0)
    fold_all(whole_units(q), side_by_side(kv, 0, HD), values, top, total, None)


STATE = [
    jax.ShapeDtypeStruct((HEADS, ROWS, HD), jnp.float32),
    jax.ShapeDtypeStruct((HEADS, ROWS, 2 * HD), jnp.float32),
]


def whole_block(shape):
    return pl.BlockSpec(shape, lambda i: (0,) * len(shape))


def attend_cache(limits, q, kv, part, state):
    count = kv.shape[0] // 4
    state_specs = [whole_block(s.shape) for s in STATE]
    return pl.pallas_call(
        functools.partial(cache_kernel, None if state is None else part * count),
        grid=(1,),
        in_specs=[
            pl.BlockSpec(memory_space=pltpu.SMEM),
            whole_block(q.shape),
            pl.BlockSpec((count,) + kv.shape[1:], lambda i: (part, 0, 0)),
        ] + ([] if state is None else state_specs),
        out_specs=state_specs,
        out_shape=STATE,
        compiler_params=pltpu.CompilerParams(vmem_limit_bytes=28 * MIB),
        cost_estimate=pl.CostEstimate(
            flops=4 * HEADS * ROWS * HD * 2048, bytes_accessed=5_000_000, transcendentals=HEADS * ROWS * 2048
        ),
    )(limits, q, kv, *([] if state is None else state))


def span_kernel(last, ahead, q, kv, *refs):
    top, total = refs[-2:]
    offset = 1 if last else 0
    top[...] = refs[offset][...]
    total[...] = refs[offset + 1][...]
    count, _, width = kv.shape
    row = lax.broadcasted_iota(jnp.int32, (ROWS, width), 0)
    slot = lax.broadcasted_iota(jnp.int32, (ROWS, width), 1)
    beyond = jnp.where(row >= SPAN_ROWS, -(1 << 24), slot - row)
    keep = jnp.concatenate([beyond <= ahead[i] for i in range(count)], axis=1)
    values = side_by_side(kv, HD, 2 * HD)
    values = jnp.concatenate([values, jnp.ones_like(values)], axis=0)
    fold_all(whole_units(q), side_by_side(kv, 0, HD), values, top, total, keep)
    if last:
        own, out = refs[0], refs[3]
        row = lax.broadcasted_iota(jnp.int32, (CAND_ROWS, CAND_ROWS), 0)
        slot = lax.broadcasted_iota(jnp.int32, (CAND_ROWS, CAND_ROWS), 1)
        values = own[HD:, :]
        values = jnp.concatenate([values, jnp.ones_like(values)], axis=0)
        units = [(h, slice(SPAN_ROWS, ROWS), q[h, SPAN_ROWS:]) for h in range(HEADS)]
        fold_all(units, own[:HD, :], values, top, total, slot <= row)
        for head in range(HEADS):
            attended = total[head, :, :HD] / total[head, :, HD:]
            out[head * HD : (head + 1) * HD, :] = attended.T.astype(jnp.bfloat16)


def attend_span(ahead, q, kv, own, state):
    last = own is not None
    state_specs = [whole_block(s.shape) for s in STATE]
    if last:
        out_specs = whole_block((HEADS * HD, ROWS))
        out_shape = jax.ShapeDtypeStruct((HEADS * HD, ROWS), jnp.bfloat16)
    else:
        out_specs, out_shape = state_specs, STATE
    return pl.pallas_call(
        functools.partial(span_kernel, last),
        grid=(1,),
        in_specs=[
            pl.BlockSpec(memory_space=pltpu.SMEM),
            whole_block(q.shape),
            whole_block(kv.shape),
        ] + ([whole_block(own.shape)] if last else []) + state_specs,
        out_specs=out_specs,
        out_shape=out_shape,
        scratch_shapes=[pltpu.VMEM(s.shape, s.dtype) for s in STATE] if last else [],
        compiler_params=pltpu.CompilerParams(vmem_limit_bytes=32 * MIB),
        cost_estimate=pl.CostEstimate(
            flops=4 * HEADS * ROWS * HD * 2048, bytes_accessed=5_000_000, transcendentals=HEADS * ROWS * 2048
        ),
    )(ahead, q, kv, *([own] if last else []), *state)


def output_kernel(picks, *refs):
    attended, (near, far), outs = refs[:NX], refs[NX : NX + 2], refs[NX + 2 :]
    for kz in range(NZ):
        ky = picks[kz]
        total = None
        for kx in range(NX):
            part = near.shape[3] // 4
            rows = jnp.concatenate(
                [
                    jnp.concatenate(
                        [half[ky, i, kx, j * part : (j + 1) * part, :] for j in range(4)], axis=1
                    )
                    for half in (near, far)
                    for i in range(2)
                ],
                axis=0,
            )
            term = jnp.dot(rows, attended[kx][...], preferred_element_type=jnp.float32)
            total = term if total is None else total + term
        outs[kz][...] = total.astype(outs[kz].dtype)


def project_out(picks, attended, near, far):
    width = near.shape[3]
    return pl.pallas_call(
        output_kernel,
        in_specs=[pl.BlockSpec(memory_space=pltpu.SMEM)] + [whole_spec()] * (NX + 2),
        out_specs=[whole_spec()] * NZ,
        out_shape=[
            jax.ShapeDtypeStruct((width, ROWS), jnp.bfloat16 if kz else jnp.float32)
            for kz in range(NZ)
        ],
        compiler_params=pltpu.CompilerParams(vmem_limit_bytes=20 * MIB),
        cost_estimate=pl.CostEstimate(
            flops=2 * ROWS * 2048 * 1280, bytes_accessed=8_000_000, transcendentals=0
        ),
    )(picks, *attended, near, far)


def join_pair(mine, other, parity):
    half = mine.shape[0] // 2
    low = jnp.where(parity == 0, mine, other)
    high = jnp.where(parity == 0, other, mine)
    return jnp.concatenate([low[:half], high[:half], low[half:], high[half:]], axis=0)


def per_device(
    span_x, cand_x, cand_len, offset, norm_gain, wq, wk, wv, q_gain, k_gain, wo, cache_k, cache_v
):
    head = lax.axis_index("head").astype(jnp.int32)
    seq = lax.axis_index("seq").astype(jnp.int32)
    at_x, at_z = head // NZ, head % NZ
    at_y, at_near, at_core = seq // 4, seq // 2 % 2, seq % 2
    parity = head % 2
    width = span_x.shape[1]
    half = HD // 2
    start = offset[0]

    part = width // 4
    own_x = jnp.concatenate([span_x.T, cand_x[0].T], axis=1)
    cache_rows = cache_k.shape[0]
    seen = (seq * cache_rows + jnp.arange(cache_rows, dtype=jnp.int32) < start)[None, :]
    keys_t, values_t = cache_k.T, cache_v.T
    cache_half = jnp.concatenate(
        [jnp.where(seen, keys_t, keys_t[:, :1]), jnp.where(seen, values_t, 0)], axis=0
    )
    other_cache = swap_pair(cache_half)
    z1, z3 = move_z(own_x, 1), move_z(own_x, 3)
    shares = []
    for kx in range(NX):
        column = ((at_x + kx) % NX * NZ * 4 + seq) * part
        share = lax.dynamic_slice(wo, (0, column), (wo.shape[0], part)).T
        shares.append(share.reshape(part, 4, HD).transpose(1, 0, 2).reshape(width, HD))
    x1 = move_x(jnp.concatenate([own_x, shares[1]], axis=1), 1)
    x3 = move_x(jnp.concatenate([own_x, shares[3]], axis=1), 3)
    to_x2 = jnp.concatenate([own_x, shares[2]], axis=1)
    to_z2, to_x2, other_cache = after((own_x, to_x2, other_cache))
    z2, x2 = move_z(to_z2, 2), move_x(to_x2, 2)
    cache_block = join_pair(cache_half, other_cache, parity)
    cache_all = lax.all_gather(cache_block, "seq")

    z1, z2, z3, x1, x2, x3 = after((z1, z2, z3, x1, x2, x3))
    stack = jnp.concatenate([z1, z2, z3], axis=0)
    x1_z, x3_z = move_x(stack, 1), move_x(stack, 3)
    x2_z2 = move_x(z2, 2)
    x2_own = x2[:, :ROWS]
    x2_z1, x2_z3 = move_z(x2_own, 1), move_z(x2_own, 3)
    wo_block = jnp.stack([shares[0], x1[:, ROWS:], x2[:, ROWS:], x3[:, ROWS:]])
    wo_near = jnp.stack([wo_block, swap_near(wo_block)])
    wo_parts = spread_y(wo_near)
    blocks = [own_x, z1, z2, z3, x1, x2, x3, x1_z, x3_z, x2_z1, x2_z2, x2_z3]
    layout = {(0, 0): (0, 0), (2, 0): (5, 0), (1, 0): (4, 0), (3, 0): (6, 0)}
    for kz in range(1, NZ):
        layout[0, kz] = (kz, 0)
        layout[1, kz], layout[3, kz] = (7, kz - 1), (8, kz - 1)
        layout[2, kz] = (8 + kz, 0)

    span_positions = start + seq * SPAN_ROWS + jnp.arange(SPAN_ROWS, dtype=jnp.int32)
    cand_positions = start + SPAN_ROWS * 4 * NY + jnp.arange(CAND_ROWS, dtype=jnp.int32)
    positions = jnp.concatenate([span_positions, cand_positions]).astype(jnp.float32)
    frequency = rope_base ** (-(jnp.arange(half, dtype=jnp.float32) * 2.0 / HD))
    angles = frequency[:, None] * positions[None, :]
    cosine, sine = jnp.cos(angles), jnp.sin(angles)
    q_cosine = jnp.concatenate([cosine, cosine], axis=0).T
    q_sine = jnp.concatenate([-sine, sine], axis=0).T

    place = jnp.stack([at_x, at_z])
    wkv_t = jnp.concatenate([wk.T, wv.T], axis=0)
    q, kv_half = project(
        layout, place, blocks, norm_gain[:, None], wq, wkv_t, q_gain[None, :], q_cosine, q_sine
    )

    def sources(core):
        return jnp.stack(
            [
                ((at_y + NY - ky) % NY * 2 + (at_near + near) % 2) * 2 + core
                for ky in range(NY)
                for near in range(2)
            ]
        )

    from_near, from_far = sources(at_core), sources(1 - at_core)
    limits = start - jnp.arange(4 * NY, dtype=jnp.int32) * cache_rows

    other_half = swap_pair(kv_half)
    state = attend_cache(limits, q, cache_all, 0, None)
    kv_new = join_pair(kv_half, other_half, parity)
    raw = kv_new[:HD].astype(jnp.float32)
    raw = raw * lax.rsqrt(jnp.mean(raw * raw, axis=0, keepdims=True) + epsilon) * k_gain[:, None]
    front, back = raw[:half], raw[half:]
    new_keys = jnp.concatenate(
        [front * cosine - back * sine, back * cosine + front * sine], axis=0
    ).astype(jnp.bfloat16)
    new_block = jnp.concatenate([new_keys, kv_new[HD:]], axis=0)
    new_block, state = after((new_block, state))
    span_block, own_block = new_block[:, :SPAN_ROWS], new_block[:, SPAN_ROWS:]
    other_near = swap_near(span_block)
    state = attend_cache(limits, q, cache_all, 1, state)
    other_near, state = after((other_near, state))
    span_parts = spread_y(jnp.stack([span_block, other_near]))
    state = attend_cache(limits, q, cache_all, 2, state)
    state = attend_cache(limits, q, cache_all, 3, state)
    span_parts, wo_parts, state = after((span_parts, wo_parts, state))
    span_near, wo_near = jnp.stack(span_parts), jnp.stack(wo_parts)
    span_far, wo_far = swap_core(span_near), swap_core(wo_near)
    span_shape = (2 * NY, 2 * HD, SPAN_ROWS)
    span_near, span_far = span_near.reshape(span_shape), span_far.reshape(span_shape)
    state = attend_span((seq - from_near) * SPAN_ROWS, q, span_near, None, state)
    attended = attend_span((seq - from_far) * SPAN_ROWS, q, span_far, own_block, state)

    a2, a1, a3 = move_x(attended, 2), move_x(attended, 1), move_x(attended, 3)
    picks = jnp.stack([(at_y - at_z - kz + 2 * NZ) % NY for kz in range(NZ)])
    pieces = project_out(picks, [attended, a1, a2, a3], wo_near, wo_far)
    result = pieces[0]
    for kz in (2, 1, 3):
        result = result + move_z(pieces[kz], kz).astype(jnp.float32)
    result = result.reshape(2, 2, part, ROWS)
    result = jnp.where(at_core == 1, result[::-1], result)
    result = jnp.where(at_near == 1, result[:, ::-1], result)
    result = result.transpose(1, 0, 2, 3).reshape(width, ROWS)
    span_out = result[:, :SPAN_ROWS].astype(jnp.bfloat16).T
    valid = jnp.arange(CAND_ROWS, dtype=jnp.int32)[None, :] < cand_len[0]
    cand_out = jnp.where(valid, result[:, SPAN_ROWS:], 0.0).astype(jnp.bfloat16).T[None]
    return span_out, cand_out


def solution(mesh):
    in_specs = (
        P("seq", "head"),
        P("seq", None, "head"),
        P("seq"),
        P(),
        P(),
        P(None, "head"),
        P(None, "head"),
        P(None, "head"),
        P(),
        P(),
        P("head", None),
        P("seq", "head"),
        P("seq", "head"),
    )
    out_specs = (P("seq", "head"), P("seq", None, "head"))
    return jax.shard_map(
        per_device, mesh=mesh, in_specs=in_specs, out_specs=out_specs, check_vma=False
    )
```

```python
import functools
import math

import jax
import jax.numpy as jnp
from jax import lax
from jax.experimental import pallas as pl
from jax.experimental.pallas import tpu as pltpu
from jax.sharding import PartitionSpec as P

epsilon = 1e-06
rope_base = 1000000.0
NX = 4
NZ = 4
HEADS = 4
HD = 128
SPAN_ROWS = 256
CAND_ROWS = 128
ROWS = SPAN_ROWS + CAND_ROWS
LOG2E = 1.4426950408889634
NY = 4
MIB = 1024 * 1024


def move_x(block, step):
    route = []
    for x in range(NX):
        for z in range(NZ):
            route.append((x * NZ + z, (x + step) % NX * NZ + z))
    return lax.ppermute(block, "head", route)


def move_z(block, step):
    route = []
    for x in range(NX):
        for z in range(NZ):
            route.append((x * NZ + z, x * NZ + (z + step) % NZ))
    return lax.ppermute(block, "head", route)


def swap_pair(block):
    return lax.ppermute(block, "head", [(h, h ^ 1) for h in range(NX * NZ)])


def move_y(block, step):
    return lax.ppermute(block, "seq", [(s, (s + 4 * step) % (4 * NY)) for s in range(4 * NY)])


def swap_near(block):
    return lax.ppermute(block, "seq", [(s, s ^ 2) for s in range(4 * NY)])


def swap_core(block):
    return lax.ppermute(block, "seq", [(s, s ^ 1) for s in range(4 * NY)])


def spread_y(near):
    others = [move_y(near, step) for step in (2, 1, 3)]
    return [near, others[1], others[0], others[2]]


def after(values, *earlier):
    return lax.optimization_barrier((values, earlier))[0]


def whole_spec():
    return pl.BlockSpec(memory_space=pltpu.VMEM)


def project_kernel(layout, place, *refs):
    count = len({ref for ref, _ in layout.values()})
    blocks = refs[:count]
    gain, wq, wkv_t, q_gain, cosine, sine, q_out, kv_out, normed = refs[count:]
    features = gain.shape[0]
    width = features // (NX * NZ)
    total = jnp.zeros((1, ROWS), jnp.float32)
    for block in blocks:
        values = block[:, :ROWS].astype(jnp.float32)
        total = total + jnp.sum(values * values, axis=0, keepdims=True)
    scale = lax.rsqrt(total / features + epsilon)
    for (kx, kz), (ref, part) in layout.items():
        x = lax.rem(place[0] + NX - kx, NX)
        z = lax.rem(place[1] + NZ - kz, NZ)
        rows = pl.ds(pl.multiple_of((x * NZ + z) * width, width), width)
        values = blocks[ref][part * width : (part + 1) * width, :ROWS].astype(jnp.float32)
        normed[rows, :] = (values * scale * gain[rows, :]).astype(jnp.bfloat16)
    kv_out[...] = jnp.dot(
        wkv_t[...], normed[...], preferred_element_type=jnp.float32
    ).astype(jnp.bfloat16)
    queries = lax.dot_general(
        normed[...], wq[...], (((0,), (0,)), ((), ())), preferred_element_type=jnp.float32
    )
    for head in range(HEADS):
        values = queries[:, head * HD : (head + 1) * HD]
        mean_square = jnp.mean(values * values, axis=1, keepdims=True)
        values = values * lax.rsqrt(mean_square + epsilon) * q_gain[...]
        turned = values * cosine[...] + pltpu.roll(values, HD // 2, 1) * sine[...]
        q_out[head] = turned.astype(jnp.bfloat16)


def project(layout, place, blocks, gain, wq, wkv_t, q_gain, cosine, sine):
    vmem = whole_spec()
    return pl.pallas_call(
        functools.partial(project_kernel, layout),
        in_specs=[pl.BlockSpec(memory_space=pltpu.SMEM)] + [vmem] * (len(blocks) + 6),
        out_specs=[vmem, vmem],
        out_shape=[
            jax.ShapeDtypeStruct((HEADS, ROWS, HD), jnp.bfloat16),
            jax.ShapeDtypeStruct((wkv_t.shape[0], ROWS), jnp.bfloat16),
        ],
        scratch_shapes=[pltpu.VMEM((wq.shape[0], ROWS), jnp.bfloat16)],
        compiler_params=pltpu.CompilerParams(vmem_limit_bytes=56 * MIB),
        cost_estimate=pl.CostEstimate(
            flops=2 * ROWS * 5120 * 640, bytes_accessed=12_000_000, transcendentals=0
        ),
    )(place, *blocks, gain, wq, wkv_t, q_gain, cosine, sine)


def fold_all(units, keys, values, top, total, keep):
    scale = LOG2E / math.sqrt(HD)
    ready = jnp.dot(units[0][2], keys, preferred_element_type=jnp.float32)
    for index, (head, rows, _) in enumerate(units):
        scores = ready * scale
        if index + 1 < len(units):
            ready = jnp.dot(units[index + 1][2], keys, preferred_element_type=jnp.float32)
        if keep is not None:
            scores = jnp.where(keep, scores, -1e30)
        old_top = top[head, rows]
        new_top = jnp.maximum(old_top, jnp.max(scores, axis=1, keepdims=True))
        factor = jnp.exp2(old_top - new_top)
        weights = jnp.exp2(scores - new_top[:, :1]).astype(jnp.bfloat16)
        added = lax.dot_general(
            weights, values, (((1,), (1,)), ((), ())), preferred_element_type=jnp.float32
        )
        total[head, rows] = total[head, rows] * jnp.concatenate([factor, factor], axis=1) + added
        top[head, rows] = new_top


def whole_units(q):
    return [(head, slice(0, ROWS), q[head]) for head in range(HEADS)]


def side_by_side(kv, low, high):
    return jnp.concatenate([kv[i, low:high, :] for i in range(kv.shape[0])], axis=1)


def cache_kernel(first, limits, q, kv, *refs):
    top, total = refs[-2:]
    if first is None:
        top[...] = jnp.full(top.shape, -1e30, jnp.float32)
        total[...] = jnp.zeros(total.shape, jnp.float32)
        first = 0
    else:
        top[...] = refs[0][...]
        total[...] = refs[1][...]
    count, _, width = kv.shape
    slot = lax.broadcasted_iota(jnp.int32, (HD, width), 1)
    counted = jnp.concatenate(
        [(slot < limits[first + i]).astype(jnp.bfloat16) for i in range(count)], axis=1
    )
    values = jnp.concatenate([side_by_side(kv, HD, 2 * HD), counted], axis=0)
    fold_all(whole_units(q), side_by_side(kv, 0, HD), values, top, total, None)


STATE = [
    jax.ShapeDtypeStruct((HEADS, ROWS, HD), jnp.float32),
    jax.ShapeDtypeStruct((HEADS, ROWS, 2 * HD), jnp.float32),
]


def whole_block(shape):
    return pl.BlockSpec(shape, lambda i: (0,) * len(shape))


def attend_cache(limits, q, kv, part, state):
    count = kv.shape[0] // 2
    state_specs = [whole_block(s.shape) for s in STATE]
    return pl.pallas_call(
        functools.partial(cache_kernel, None if state is None else part * count),
        grid=(1,),
        in_specs=[
            pl.BlockSpec(memory_space=pltpu.SMEM),
            whole_block(q.shape),
            pl.BlockSpec((count,) + kv.shape[1:], lambda i: (part, 0, 0)),
        ] + ([] if state is None else state_specs),
        out_specs=state_specs,
        out_shape=STATE,
        compiler_params=pltpu.CompilerParams(vmem_limit_bytes=28 * MIB),
        cost_estimate=pl.CostEstimate(
            flops=4 * HEADS * ROWS * HD * 2048, bytes_accessed=5_000_000, transcendentals=HEADS * ROWS * 2048
        ),
    )(limits, q, kv, *([] if state is None else state))


def span_kernel(last, ahead, q, kv, *refs):
    top, total = refs[-2:]
    offset = 1 if last else 0
    top[...] = refs[offset][...]
    total[...] = refs[offset + 1][...]
    count, _, width = kv.shape
    row = lax.broadcasted_iota(jnp.int32, (ROWS, width), 0)
    slot = lax.broadcasted_iota(jnp.int32, (ROWS, width), 1)
    beyond = jnp.where(row >= SPAN_ROWS, -(1 << 24), slot - row)
    keep = jnp.concatenate([beyond <= ahead[i] for i in range(count)], axis=1)
    values = side_by_side(kv, HD, 2 * HD)
    values = jnp.concatenate([values, jnp.ones_like(values)], axis=0)
    fold_all(whole_units(q), side_by_side(kv, 0, HD), values, top, total, keep)
    if last:
        own, out = refs[0], refs[3]
        row = lax.broadcasted_iota(jnp.int32, (CAND_ROWS, CAND_ROWS), 0)
        slot = lax.broadcasted_iota(jnp.int32, (CAND_ROWS, CAND_ROWS), 1)
        values = own[HD:, :]
        values = jnp.concatenate([values, jnp.ones_like(values)], axis=0)
        units = [(h, slice(SPAN_ROWS, ROWS), q[h, SPAN_ROWS:]) for h in range(HEADS)]
        fold_all(units, own[:HD, :], values, top, total, slot <= row)
        for head in range(HEADS):
            attended = total[head, :, :HD] / total[head, :, HD:]
            out[head * HD : (head + 1) * HD, :] = attended.T.astype(jnp.bfloat16)


def attend_span(ahead, q, kv, own, state):
    last = own is not None
    state_specs = [whole_block(s.shape) for s in STATE]
    if last:
        out_specs = whole_block((HEADS * HD, ROWS))
        out_shape = jax.ShapeDtypeStruct((HEADS * HD, ROWS), jnp.bfloat16)
    else:
        out_specs, out_shape = state_specs, STATE
    return pl.pallas_call(
        functools.partial(span_kernel, last),
        grid=(1,),
        in_specs=[
            pl.BlockSpec(memory_space=pltpu.SMEM),
            whole_block(q.shape),
            whole_block(kv.shape),
        ] + ([whole_block(own.shape)] if last else []) + state_specs,
        out_specs=out_specs,
        out_shape=out_shape,
        scratch_shapes=[pltpu.VMEM(s.shape, s.dtype) for s in STATE] if last else [],
        compiler_params=pltpu.CompilerParams(vmem_limit_bytes=32 * MIB),
        cost_estimate=pl.CostEstimate(
            flops=4 * HEADS * ROWS * HD * 2048, bytes_accessed=5_000_000, transcendentals=HEADS * ROWS * 2048
        ),
    )(ahead, q, kv, *([own] if last else []), *state)


def output_kernel(picks, *refs):
    attended, (near, far), outs = refs[:NX], refs[NX : NX + 2], refs[NX + 2 :]
    for kz in range(NZ):
        ky = picks[kz]
        total = None
        for kx in range(NX):
            part = near.shape[3] // 4
            rows = jnp.concatenate(
                [
                    jnp.concatenate(
                        [half[ky, i, kx, j * part : (j + 1) * part, :] for j in range(4)], axis=1
                    )
                    for half in (near, far)
                    for i in range(2)
                ],
                axis=0,
            )
            term = jnp.dot(rows, attended[kx][...], preferred_element_type=jnp.float32)
            total = term if total is None else total + term
        outs[kz][...] = total.astype(outs[kz].dtype)


def project_out(picks, attended, near, far):
    width = near.shape[3]
    return pl.pallas_call(
        output_kernel,
        in_specs=[pl.BlockSpec(memory_space=pltpu.SMEM)] + [whole_spec()] * (NX + 2),
        out_specs=[whole_spec()] * NZ,
        out_shape=[
            jax.ShapeDtypeStruct((width, ROWS), jnp.bfloat16 if kz else jnp.float32)
            for kz in range(NZ)
        ],
        compiler_params=pltpu.CompilerParams(vmem_limit_bytes=20 * MIB),
        cost_estimate=pl.CostEstimate(
            flops=2 * ROWS * 2048 * 1280, bytes_accessed=8_000_000, transcendentals=0
        ),
    )(picks, *attended, near, far)


def join_pair(mine, other, parity):
    half = mine.shape[0] // 2
    low = jnp.where(parity == 0, mine, other)
    high = jnp.where(parity == 0, other, mine)
    return jnp.concatenate([low[:half], high[:half], low[half:], high[half:]], axis=0)


def per_device(
    span_x, cand_x, cand_len, offset, norm_gain, wq, wk, wv, q_gain, k_gain, wo, cache_k, cache_v
):
    head = lax.axis_index("head").astype(jnp.int32)
    seq = lax.axis_index("seq").astype(jnp.int32)
    at_x, at_z = head // NZ, head % NZ
    at_y, at_near, at_core = seq // 4, seq // 2 % 2, seq % 2
    parity = head % 2
    width = span_x.shape[1]
    half = HD // 2
    start = offset[0]

    part = width // 4
    own_x = jnp.concatenate([span_x.T, cand_x[0].T], axis=1)
    cache_rows = cache_k.shape[0]
    seen = (seq * cache_rows + jnp.arange(cache_rows, dtype=jnp.int32) < start)[None, :]
    keys_t, values_t = cache_k.T, cache_v.T
    cache_half = jnp.concatenate(
        [jnp.where(seen, keys_t, keys_t[:, :1]), jnp.where(seen, values_t, 0)], axis=0
    )
    z1, z3 = move_z(own_x, 1), move_z(own_x, 3)
    other_cache = swap_pair(cache_half)
    shares = []
    for kx in range(NX):
        column = ((at_x + kx) % NX * NZ * 4 + seq) * part
        share = lax.dynamic_slice(wo, (0, column), (wo.shape[0], part)).T
        shares.append(share.reshape(part, 4, HD).transpose(1, 0, 2).reshape(width, HD))
    x1 = move_x(jnp.concatenate([own_x, shares[1]], axis=1), 1)
    x3 = move_x(jnp.concatenate([own_x, shares[3]], axis=1), 3)
    to_x2 = jnp.concatenate([own_x, shares[2]], axis=1)

    z1, z3, x1, x3, other_cache, to_x2, to_z2 = after(
        (z1, z3, x1, x3, other_cache, to_x2, own_x)
    )
    cache_block = join_pair(cache_half, other_cache, parity)
    other_near = swap_near(cache_block)
    z2 = move_z(to_z2, 2)
    pair = jnp.concatenate([z1, z3], axis=0)
    x1_pair, x3_pair = move_x(pair, 1), move_x(pair, 3)
    x2 = move_x(to_x2, 2)

    z2, x1_pair, x3_pair, x2, other_near = after((z2, x1_pair, x3_pair, x2, other_near))
    cache_near = jnp.stack([cache_block, other_near])
    x2_z = move_x(jnp.concatenate([pair, z2], axis=0), 2)
    x1_z2 = move_x(z2, 1)
    y1, y3, y2 = move_y(cache_near, 1), move_y(cache_near, 3), move_y(cache_near, 2)
    to_x3, y1 = after((z2, y1))
    x3_z2 = move_x(to_x3, 3)
    cache_parts = [cache_near, y1, y2, y3]
    wo_block = jnp.stack([shares[0], x1[:, ROWS:], x2[:, ROWS:], x3[:, ROWS:]])
    wo_near = jnp.stack([wo_block, swap_near(wo_block)])
    x1_z2, x2_z, x3_z2, cache_parts, wo_near = after((x1_z2, x2_z, x3_z2, cache_parts, wo_near))
    wo_parts = spread_y(wo_near)
    blocks = [own_x, z1, z3, z2, x1, x2, x3, x1_pair, x3_pair, x1_z2, x3_z2, x2_z]
    layout = {(0, 0): (0, 0), (0, 1): (1, 0), (0, 3): (2, 0), (0, 2): (3, 0)}
    layout.update({(1, 0): (4, 0), (2, 0): (5, 0), (3, 0): (6, 0)})
    layout.update({(1, 1): (7, 0), (1, 3): (7, 1), (3, 1): (8, 0), (3, 3): (8, 1)})
    layout.update({(1, 2): (9, 0), (3, 2): (10, 0)})
    layout.update({(2, 1): (11, 0), (2, 3): (11, 1), (2, 2): (11, 2)})

    span_positions = start + seq * SPAN_ROWS + jnp.arange(SPAN_ROWS, dtype=jnp.int32)
    cand_positions = start + SPAN_ROWS * 4 * NY + jnp.arange(CAND_ROWS, dtype=jnp.int32)
    positions = jnp.concatenate([span_positions, cand_positions]).astype(jnp.float32)
    frequency = rope_base ** (-(jnp.arange(half, dtype=jnp.float32) * 2.0 / HD))
    angles = frequency[:, None] * positions[None, :]
    cosine, sine = jnp.cos(angles), jnp.sin(angles)
    q_cosine = jnp.concatenate([cosine, cosine], axis=0).T
    q_sine = jnp.concatenate([-sine, sine], axis=0).T

    place = jnp.stack([at_x, at_z])
    wkv_t = jnp.concatenate([wk.T, wv.T], axis=0)
    q, kv_half = project(
        layout, place, blocks, norm_gain[:, None], wq, wkv_t, q_gain[None, :], q_cosine, q_sine
    )

    def sources(core):
        return jnp.stack(
            [
                ((at_y + NY - ky) % NY * 2 + (at_near + near) % 2) * 2 + core
                for ky in range(NY)
                for near in range(2)
            ]
        )

    from_near, from_far = sources(at_core), sources(1 - at_core)
    near_limits = start - from_near * cache_rows
    far_limits = start - from_far * cache_rows
    cache_near = jnp.stack(cache_parts)
    cache_far = swap_core(cache_near)
    cache_shape = (2 * NY, 2 * HD, cache_rows)
    cache_near, cache_far = cache_near.reshape(cache_shape), cache_far.reshape(cache_shape)

    other_half = swap_pair(kv_half)
    state = attend_cache(near_limits, q, cache_near, 0, None)
    kv_new = join_pair(kv_half, other_half, parity)
    raw = kv_new[:HD].astype(jnp.float32)
    raw = raw * lax.rsqrt(jnp.mean(raw * raw, axis=0, keepdims=True) + epsilon) * k_gain[:, None]
    front, back = raw[:half], raw[half:]
    new_keys = jnp.concatenate(
        [front * cosine - back * sine, back * cosine + front * sine], axis=0
    ).astype(jnp.bfloat16)
    new_block = jnp.concatenate([new_keys, kv_new[HD:]], axis=0)
    new_block, state = after((new_block, state))
    span_block, own_block = new_block[:, :SPAN_ROWS], new_block[:, SPAN_ROWS:]
    other_near = swap_near(span_block)
    state = attend_cache(near_limits, q, cache_near, 1, state)
    other_near, state, cache_far, wo_parts = after((other_near, state, cache_far, wo_parts))
    span_parts = spread_y(jnp.stack([span_block, other_near]))
    state = attend_cache(far_limits, q, cache_far, 0, state)
    state = attend_cache(far_limits, q, cache_far, 1, state)
    span_parts, state = after((span_parts, state))
    span_near, wo_near = jnp.stack(span_parts), jnp.stack(wo_parts)
    span_far, wo_far = swap_core(span_near), swap_core(wo_near)
    span_shape = (2 * NY, 2 * HD, SPAN_ROWS)
    span_near, span_far = span_near.reshape(span_shape), span_far.reshape(span_shape)
    state = attend_span((seq - from_near) * SPAN_ROWS, q, span_near, None, state)
    attended = attend_span((seq - from_far) * SPAN_ROWS, q, span_far, own_block, state)

    a2, a1, a3 = move_x(attended, 2), move_x(attended, 1), move_x(attended, 3)
    picks = jnp.stack([(at_y - at_z - kz + 2 * NZ) % NY for kz in range(NZ)])
    pieces = project_out(picks, [attended, a1, a2, a3], wo_near, wo_far)
    result = pieces[0]
    for kz in (2, 1, 3):
        result = result + move_z(pieces[kz], kz).astype(jnp.float32)
    result = result.reshape(2, 2, part, ROWS)
    result = jnp.where(at_core == 1, result[::-1], result)
    result = jnp.where(at_near == 1, result[:, ::-1], result)
    result = result.transpose(1, 0, 2, 3).reshape(width, ROWS)
    span_out = result[:, :SPAN_ROWS].astype(jnp.bfloat16).T
    valid = jnp.arange(CAND_ROWS, dtype=jnp.int32)[None, :] < cand_len[0]
    cand_out = jnp.where(valid, result[:, SPAN_ROWS:], 0.0).astype(jnp.bfloat16).T[None]
    return span_out, cand_out


def solution(mesh):
    in_specs = (
        P("seq", "head"),
        P("seq", None, "head"),
        P("seq"),
        P(),
        P(),
        P(None, "head"),
        P(None, "head"),
        P(None, "head"),
        P(),
        P(),
        P("head", None),
        P("seq", "head"),
        P("seq", "head"),
    )
    out_specs = (P("seq", "head"), P("seq", None, "head"))
    return jax.shard_map(
        per_device, mesh=mesh, in_specs=in_specs, out_specs=out_specs, check_vma=False
    )
```

```python
import functools
import math

import jax
import jax.numpy as jnp
from jax import lax
from jax.experimental import pallas as pl
from jax.experimental.pallas import tpu as pltpu
from jax.sharding import PartitionSpec as P

epsilon = 1e-06
rope_base = 1000000.0
NX = 4
NZ = 4
HEADS = 4
HD = 128
SPAN_ROWS = 256
CAND_ROWS = 128
ROWS = SPAN_ROWS + CAND_ROWS
LOG2E = 1.4426950408889634
NY = 4
MIB = 1024 * 1024


def move_x(block, step):
    route = []
    for x in range(NX):
        for z in range(NZ):
            route.append((x * NZ + z, (x + step) % NX * NZ + z))
    return lax.ppermute(block, "head", route)


def move_z(block, step):
    route = []
    for x in range(NX):
        for z in range(NZ):
            route.append((x * NZ + z, x * NZ + (z + step) % NZ))
    return lax.ppermute(block, "head", route)


def swap_pair(block):
    return lax.ppermute(block, "head", [(h, h ^ 1) for h in range(NX * NZ)])


def move_y(block, step):
    return lax.ppermute(block, "seq", [(s, (s + 4 * step) % (4 * NY)) for s in range(4 * NY)])


def swap_near(block):
    return lax.ppermute(block, "seq", [(s, s ^ 2) for s in range(4 * NY)])


def swap_core(block):
    return lax.ppermute(block, "seq", [(s, s ^ 1) for s in range(4 * NY)])


def spread_y(near):
    others = [move_y(near, step) for step in (2, 1, 3)]
    return [near, others[1], others[0], others[2]]


def after(values, *earlier):
    return lax.optimization_barrier((values, earlier))[0]


def whole_spec():
    return pl.BlockSpec(memory_space=pltpu.VMEM)


def project_kernel(layout, place, *refs):
    count = len({ref for ref, _ in layout.values()})
    blocks = refs[:count]
    gain, wq, wkv_t, q_gain, cosine, sine, q_out, kv_out, normed = refs[count:]
    features = gain.shape[0]
    width = features // (NX * NZ)
    total = jnp.zeros((1, ROWS), jnp.float32)
    for block in blocks:
        values = block[:, :ROWS].astype(jnp.float32)
        total = total + jnp.sum(values * values, axis=0, keepdims=True)
    scale = lax.rsqrt(total / features + epsilon)
    for (kx, kz), (ref, part) in layout.items():
        x = lax.rem(place[0] + NX - kx, NX)
        z = lax.rem(place[1] + NZ - kz, NZ)
        rows = pl.ds(pl.multiple_of((x * NZ + z) * width, width), width)
        values = blocks[ref][part * width : (part + 1) * width, :ROWS].astype(jnp.float32)
        normed[rows, :] = (values * scale * gain[rows, :]).astype(jnp.bfloat16)
    kv_out[...] = jnp.dot(
        wkv_t[...], normed[...], preferred_element_type=jnp.float32
    ).astype(jnp.bfloat16)
    queries = lax.dot_general(
        normed[...], wq[...], (((0,), (0,)), ((), ())), preferred_element_type=jnp.float32
    )
    for head in range(HEADS):
        values = queries[:, head * HD : (head + 1) * HD]
        mean_square = jnp.mean(values * values, axis=1, keepdims=True)
        values = values * lax.rsqrt(mean_square + epsilon) * q_gain[...]
        turned = values * cosine[...] + pltpu.roll(values, HD // 2, 1) * sine[...]
        q_out[head] = turned.astype(jnp.bfloat16)


def project(layout, place, blocks, gain, wq, wkv_t, q_gain, cosine, sine):
    vmem = whole_spec()
    return pl.pallas_call(
        functools.partial(project_kernel, layout),
        in_specs=[pl.BlockSpec(memory_space=pltpu.SMEM)] + [vmem] * (len(blocks) + 6),
        out_specs=[vmem, vmem],
        out_shape=[
            jax.ShapeDtypeStruct((HEADS, ROWS, HD), jnp.bfloat16),
            jax.ShapeDtypeStruct((wkv_t.shape[0], ROWS), jnp.bfloat16),
        ],
        scratch_shapes=[pltpu.VMEM((wq.shape[0], ROWS), jnp.bfloat16)],
        compiler_params=pltpu.CompilerParams(vmem_limit_bytes=56 * MIB),
        cost_estimate=pl.CostEstimate(
            flops=2 * ROWS * 5120 * 640, bytes_accessed=12_000_000, transcendentals=0
        ),
    )(place, *blocks, gain, wq, wkv_t, q_gain, cosine, sine)


def fold_all(units, keys, values, top, total, keep):
    scale = LOG2E / math.sqrt(HD)
    ready = jnp.dot(units[0][2], keys, preferred_element_type=jnp.float32)
    for index, (head, rows, _) in enumerate(units):
        scores = ready * scale
        if index + 1 < len(units):
            ready = jnp.dot(units[index + 1][2], keys, preferred_element_type=jnp.float32)
        if keep is not None:
            scores = jnp.where(keep, scores, -1e30)
        old_top = top[head, rows]
        new_top = jnp.maximum(old_top, jnp.max(scores, axis=1, keepdims=True))
        factor = jnp.exp2(old_top - new_top)
        weights = jnp.exp2(scores - new_top[:, :1]).astype(jnp.bfloat16)
        added = lax.dot_general(
            weights, values, (((1,), (1,)), ((), ())), preferred_element_type=jnp.float32
        )
        total[head, rows] = total[head, rows] * jnp.concatenate([factor, factor], axis=1) + added
        top[head, rows] = new_top


def whole_units(q):
    return [(head, slice(0, ROWS), q[head]) for head in range(HEADS)]


def side_by_side(kv, low, high):
    return jnp.concatenate([kv[i, low:high, :] for i in range(kv.shape[0])], axis=1)


def cache_kernel(first, limits, q, kv, *refs):
    top, total = refs[-2:]
    if first is None:
        top[...] = jnp.full(top.shape, -1e30, jnp.float32)
        total[...] = jnp.zeros(total.shape, jnp.float32)
        first = 0
    else:
        top[...] = refs[0][...]
        total[...] = refs[1][...]
    count, _, width = kv.shape
    slot = lax.broadcasted_iota(jnp.int32, (HD, width), 1)
    counted = jnp.concatenate(
        [(slot < limits[first + i]).astype(jnp.bfloat16) for i in range(count)], axis=1
    )
    values = jnp.concatenate([side_by_side(kv, HD, 2 * HD), counted], axis=0)
    fold_all(whole_units(q), side_by_side(kv, 0, HD), values, top, total, None)


STATE = [
    jax.ShapeDtypeStruct((HEADS, ROWS, HD), jnp.float32),
    jax.ShapeDtypeStruct((HEADS, ROWS, 2 * HD), jnp.float32),
]


def whole_block(shape):
    return pl.BlockSpec(shape, lambda i: (0,) * len(shape))


def attend_cache(limits, q, kv, part, state):
    count = kv.shape[0] // 2
    state_specs = [whole_block(s.shape) for s in STATE]
    return pl.pallas_call(
        functools.partial(cache_kernel, None if state is None else part * count),
        grid=(1,),
        in_specs=[
            pl.BlockSpec(memory_space=pltpu.SMEM),
            whole_block(q.shape),
            pl.BlockSpec((count,) + kv.shape[1:], lambda i: (part, 0, 0)),
        ] + ([] if state is None else state_specs),
        out_specs=state_specs,
        out_shape=STATE,
        compiler_params=pltpu.CompilerParams(vmem_limit_bytes=28 * MIB),
        cost_estimate=pl.CostEstimate(
            flops=4 * HEADS * ROWS * HD * 2048, bytes_accessed=5_000_000, transcendentals=HEADS * ROWS * 2048
        ),
    )(limits, q, kv, *([] if state is None else state))


def span_kernel(last, ahead, q, kv, *refs):
    top, total = refs[-2:]
    offset = 1 if last else 0
    top[...] = refs[offset][...]
    total[...] = refs[offset + 1][...]
    count, _, width = kv.shape
    row = lax.broadcasted_iota(jnp.int32, (ROWS, width), 0)
    slot = lax.broadcasted_iota(jnp.int32, (ROWS, width), 1)
    beyond = jnp.where(row >= SPAN_ROWS, -(1 << 24), slot - row)
    keep = jnp.concatenate([beyond <= ahead[i] for i in range(count)], axis=1)
    values = side_by_side(kv, HD, 2 * HD)
    values = jnp.concatenate([values, jnp.ones_like(values)], axis=0)
    fold_all(whole_units(q), side_by_side(kv, 0, HD), values, top, total, keep)
    if last:
        own, out = refs[0], refs[3]
        row = lax.broadcasted_iota(jnp.int32, (CAND_ROWS, CAND_ROWS), 0)
        slot = lax.broadcasted_iota(jnp.int32, (CAND_ROWS, CAND_ROWS), 1)
        values = own[HD:, :]
        values = jnp.concatenate([values, jnp.ones_like(values)], axis=0)
        units = [(h, slice(SPAN_ROWS, ROWS), q[h, SPAN_ROWS:]) for h in range(HEADS)]
        fold_all(units, own[:HD, :], values, top, total, slot <= row)
        for head in range(HEADS):
            attended = total[head, :, :HD] / total[head, :, HD:]
            out[head * HD : (head + 1) * HD, :] = attended.T.astype(jnp.bfloat16)


def attend_span(ahead, q, kv, own, state):
    last = own is not None
    state_specs = [whole_block(s.shape) for s in STATE]
    if last:
        out_specs = whole_block((HEADS * HD, ROWS))
        out_shape = jax.ShapeDtypeStruct((HEADS * HD, ROWS), jnp.bfloat16)
    else:
        out_specs, out_shape = state_specs, STATE
    return pl.pallas_call(
        functools.partial(span_kernel, last),
        grid=(1,),
        in_specs=[
            pl.BlockSpec(memory_space=pltpu.SMEM),
            whole_block(q.shape),
            whole_block(kv.shape),
        ] + ([whole_block(own.shape)] if last else []) + state_specs,
        out_specs=out_specs,
        out_shape=out_shape,
        scratch_shapes=[pltpu.VMEM(s.shape, s.dtype) for s in STATE] if last else [],
        compiler_params=pltpu.CompilerParams(vmem_limit_bytes=32 * MIB),
        cost_estimate=pl.CostEstimate(
            flops=4 * HEADS * ROWS * HD * 2048, bytes_accessed=5_000_000, transcendentals=HEADS * ROWS * 2048
        ),
    )(ahead, q, kv, *([own] if last else []), *state)


def output_kernel(picks, *refs):
    attended, (near, far), outs = refs[:NX], refs[NX : NX + 2], refs[NX + 2 :]
    for kz in range(NZ):
        ky = picks[kz]
        total = None
        for kx in range(NX):
            part = near.shape[3] // 4
            rows = jnp.concatenate(
                [
                    jnp.concatenate(
                        [half[ky, i, kx, j * part : (j + 1) * part, :] for j in range(4)], axis=1
                    )
                    for half in (near, far)
                    for i in range(2)
                ],
                axis=0,
            )
            term = jnp.dot(rows, attended[kx][...], preferred_element_type=jnp.float32)
            total = term if total is None else total + term
        outs[kz][...] = total.astype(outs[kz].dtype)


def project_out(picks, attended, near, far):
    width = near.shape[3]
    return pl.pallas_call(
        output_kernel,
        in_specs=[pl.BlockSpec(memory_space=pltpu.SMEM)] + [whole_spec()] * (NX + 2),
        out_specs=[whole_spec()] * NZ,
        out_shape=[
            jax.ShapeDtypeStruct((width, ROWS), jnp.bfloat16 if kz else jnp.float32)
            for kz in range(NZ)
        ],
        compiler_params=pltpu.CompilerParams(vmem_limit_bytes=20 * MIB),
        cost_estimate=pl.CostEstimate(
            flops=2 * ROWS * 2048 * 1280, bytes_accessed=8_000_000, transcendentals=0
        ),
    )(picks, *attended, near, far)


def join_pair(mine, other, parity):
    half = mine.shape[0] // 2
    low = jnp.where(parity == 0, mine, other)
    high = jnp.where(parity == 0, other, mine)
    return jnp.concatenate([low[:half], high[:half], low[half:], high[half:]], axis=0)


def per_device(
    span_x, cand_x, cand_len, offset, norm_gain, wq, wk, wv, q_gain, k_gain, wo, cache_k, cache_v
):
    head = lax.axis_index("head").astype(jnp.int32)
    seq = lax.axis_index("seq").astype(jnp.int32)
    at_x, at_z = head // NZ, head % NZ
    at_y, at_near, at_core = seq // 4, seq // 2 % 2, seq % 2
    parity = head % 2
    width = span_x.shape[1]
    half = HD // 2
    start = offset[0]

    part = width // 4
    own_x = jnp.concatenate([span_x.T, cand_x[0].T], axis=1)
    cache_rows = cache_k.shape[0]
    seen = (seq * cache_rows + jnp.arange(cache_rows, dtype=jnp.int32) < start)[None, :]
    keys_t, values_t = cache_k.T, cache_v.T
    cache_half = jnp.concatenate(
        [jnp.where(seen, keys_t, keys_t[:, :1]), jnp.where(seen, values_t, 0)], axis=0
    )
    z1, z3 = move_z(own_x, 1), move_z(own_x, 3)
    other_cache = swap_pair(cache_half)
    shares = []
    for kx in range(NX):
        column = ((at_x + kx) % NX * NZ * 4 + seq) * part
        share = lax.dynamic_slice(wo, (0, column), (wo.shape[0], part)).T
        shares.append(share.reshape(part, 4, HD).transpose(1, 0, 2).reshape(width, HD))
    x1 = move_x(jnp.concatenate([own_x, shares[1]], axis=1), 1)
    x3 = move_x(jnp.concatenate([own_x, shares[3]], axis=1), 3)
    to_x2 = jnp.concatenate([own_x, shares[2]], axis=1)

    z1, z3, x1, x3, other_cache, to_x2, to_z2 = after(
        (z1, z3, x1, x3, other_cache, to_x2, own_x)
    )
    cache_block = join_pair(cache_half, other_cache, parity)
    other_near = swap_near(cache_block)
    z2 = move_z(to_z2, 2)
    pair = jnp.concatenate([z1, z3], axis=0)
    x1_pair, x3_pair = move_x(pair, 1), move_x(pair, 3)
    x2 = move_x(to_x2, 2)

    z2, x1_pair, x3_pair, x2, other_near = after((z2, x1_pair, x3_pair, x2, other_near))
    cache_near = jnp.stack([cache_block, other_near])
    x2_z = move_x(jnp.concatenate([pair, z2], axis=0), 2)
    x1_z2 = move_x(z2, 1)
    y1, y3, y2 = move_y(cache_near, 1), move_y(cache_near, 3), move_y(cache_near, 2)
    to_x3, y1 = after((z2, y1))
    x3_z2 = move_x(to_x3, 3)
    cache_parts = [cache_near, y1, y2, y3]
    wo_block = jnp.stack([shares[0], x1[:, ROWS:], x2[:, ROWS:], x3[:, ROWS:]])
    wo_near = jnp.stack([wo_block, swap_near(wo_block)])
    blocks = [own_x, z1, z3, z2, x1, x2, x3, x1_pair, x3_pair, x1_z2, x3_z2, x2_z]
    layout = {(0, 0): (0, 0), (0, 1): (1, 0), (0, 3): (2, 0), (0, 2): (3, 0)}
    layout.update({(1, 0): (4, 0), (2, 0): (5, 0), (3, 0): (6, 0)})
    layout.update({(1, 1): (7, 0), (1, 3): (7, 1), (3, 1): (8, 0), (3, 3): (8, 1)})
    layout.update({(1, 2): (9, 0), (3, 2): (10, 0)})
    layout.update({(2, 1): (11, 0), (2, 3): (11, 1), (2, 2): (11, 2)})

    span_positions = start + seq * SPAN_ROWS + jnp.arange(SPAN_ROWS, dtype=jnp.int32)
    cand_positions = start + SPAN_ROWS * 4 * NY + jnp.arange(CAND_ROWS, dtype=jnp.int32)
    positions = jnp.concatenate([span_positions, cand_positions]).astype(jnp.float32)
    frequency = rope_base ** (-(jnp.arange(half, dtype=jnp.float32) * 2.0 / HD))
    angles = frequency[:, None] * positions[None, :]
    cosine, sine = jnp.cos(angles), jnp.sin(angles)
    q_cosine = jnp.concatenate([cosine, cosine], axis=0).T
    q_sine = jnp.concatenate([-sine, sine], axis=0).T

    place = jnp.stack([at_x, at_z])
    wkv_t = jnp.concatenate([wk.T, wv.T], axis=0)
    q, kv_half = project(
        layout, place, blocks, norm_gain[:, None], wq, wkv_t, q_gain[None, :], q_cosine, q_sine
    )

    def sources(core):
        return jnp.stack(
            [
                ((at_y + NY - ky) % NY * 2 + (at_near + near) % 2) * 2 + core
                for ky in range(NY)
                for near in range(2)
            ]
        )

    from_near, from_far = sources(at_core), sources(1 - at_core)
    near_limits = start - from_near * cache_rows
    far_limits = start - from_far * cache_rows
    cache_parts, wo_near = after((cache_parts, wo_near), kv_half)
    wo_parts = spread_y(wo_near)
    cache_near = jnp.stack(cache_parts)
    cache_far = swap_core(cache_near)
    cache_shape = (2 * NY, 2 * HD, cache_rows)
    cache_near, cache_far = cache_near.reshape(cache_shape), cache_far.reshape(cache_shape)

    other_half = swap_pair(kv_half)
    state = attend_cache(near_limits, q, cache_near, 0, None)
    kv_new = join_pair(kv_half, other_half, parity)
    raw = kv_new[:HD].astype(jnp.float32)
    raw = raw * lax.rsqrt(jnp.mean(raw * raw, axis=0, keepdims=True) + epsilon) * k_gain[:, None]
    front, back = raw[:half], raw[half:]
    new_keys = jnp.concatenate(
        [front * cosine - back * sine, back * cosine + front * sine], axis=0
    ).astype(jnp.bfloat16)
    new_block = jnp.concatenate([new_keys, kv_new[HD:]], axis=0)
    new_block, state = after((new_block, state))
    span_block, own_block = new_block[:, :SPAN_ROWS], new_block[:, SPAN_ROWS:]
    other_near = swap_near(span_block)
    state = attend_cache(near_limits, q, cache_near, 1, state)
    other_near, state, cache_far, wo_parts[1] = after(
        (other_near, state, cache_far, wo_parts[1])
    )
    span_parts = spread_y(jnp.stack([span_block, other_near]))
    state = attend_cache(far_limits, q, cache_far, 0, state)
    state = attend_cache(far_limits, q, cache_far, 1, state)
    span_parts, state, wo_parts = after((span_parts, state, wo_parts))
    span_near, wo_near = jnp.stack(span_parts), jnp.stack(wo_parts)
    span_far, wo_far = swap_core(span_near), swap_core(wo_near)
    span_shape = (2 * NY, 2 * HD, SPAN_ROWS)
    span_near, span_far = span_near.reshape(span_shape), span_far.reshape(span_shape)
    state = attend_span((seq - from_near) * SPAN_ROWS, q, span_near, None, state)
    attended = attend_span((seq - from_far) * SPAN_ROWS, q, span_far, own_block, state)

    a2, a1, a3 = move_x(attended, 2), move_x(attended, 1), move_x(attended, 3)
    picks = jnp.stack([(at_y - at_z - kz + 2 * NZ) % NY for kz in range(NZ)])
    pieces = project_out(picks, [attended, a1, a2, a3], wo_near, wo_far)
    result = pieces[0]
    for kz in (2, 1, 3):
        result = result + move_z(pieces[kz], kz).astype(jnp.float32)
    result = result.reshape(2, 2, part, ROWS)
    result = jnp.where(at_core == 1, result[::-1], result)
    result = jnp.where(at_near == 1, result[:, ::-1], result)
    result = result.transpose(1, 0, 2, 3).reshape(width, ROWS)
    span_out = result[:, :SPAN_ROWS].astype(jnp.bfloat16).T
    valid = jnp.arange(CAND_ROWS, dtype=jnp.int32)[None, :] < cand_len[0]
    cand_out = jnp.where(valid, result[:, SPAN_ROWS:], 0.0).astype(jnp.bfloat16).T[None]
    return span_out, cand_out


def solution(mesh):
    in_specs = (
        P("seq", "head"),
        P("seq", None, "head"),
        P("seq"),
        P(),
        P(),
        P(None, "head"),
        P(None, "head"),
        P(None, "head"),
        P(),
        P(),
        P("head", None),
        P("seq", "head"),
        P("seq", "head"),
    )
    out_specs = (P("seq", "head"), P("seq", None, "head"))
    return jax.shard_map(
        per_device, mesh=mesh, in_specs=in_specs, out_specs=out_specs, check_vma=False
    )
```
